128 devices in a mesh: grp: 4 (over x), sta: 32 (over z, y, core).
Axes of the slice: x: 4, y: 4, z: 4, core: 2. Of those that a mesh axis runs over, the one named last changes fastest.
Arguments:
- spectra: float32 [1024, 2, 18432], P(('grp', 'sta')), may hold values from -61 to 61
- stacks: float32 [12288, 1601], P(('grp', 'sta')), may hold values from -6 to 6
- pair_sta: int32 [2, 12288], P(None, ('grp', 'sta')), may hold values from 0 to 255
- pair_valid: int32 [12288], P(('grp', 'sta')), may hold values 0 or 1
- owner: int32 [12288, 1], P(('grp', 'sta')), may hold values from 0 to 127; in each aligned block of 96 rows (0 to 95, 96 to 191, ...) at most 2 rows name the same one
- slot: int32 [12288], P(('grp', 'sta')), may hold values from 0 to 95
Outputs:
- stacks_new: float32 [12288, 1601], P(('grp', 'sta'))
The draws below stay inside these ranges and needn't reach their ends.
Inputs may be any that keep to these rules, and one draw needn't show every extreme that they name: Among the 96 rows of one device no owner is named more than 2 times.
All inputs are finite; a program needn't handle non-finite values. No bound on the sum of `pair_valid` on one device may be relied on, other than what follows from the above.
Results may differ from the reference program's by a relative error of at most 0.0041.
Values may be sent and summed in bfloat16 or wider, within the bound.
A program may use at most 128 MiB of HBM per device.

```python
import math
import jax
import jax.numpy as jnp
import numpy as np
from jax import lax

F = 18432
BAND = 64
LAGS = 1601
P_DEV = 96
CAP = 2
STK_DEV = 96
GSTA = 256
STATIONS = 1024
PAIRS = 12288
STACKS = 12288
N_STA = 32
DEVICES = 128


def draw_spectra(key, part):
    key_base, key_scale = jax.random.split(jax.random.fold_in(key, 17))
    base = jnp.clip(jax.random.normal(key_base, (STATIONS, 2, F // BAND, BAND), jnp.float32), -5.0, 5.0)
    level = jax.random.uniform(key_scale, (STATIONS, 1, F // BAND, 1), jnp.float32, -1.5, 1.5)
    return (base * jnp.exp(level)).reshape(STATIONS, 2, F)


def plant(values, key, least, largest):
    longest = values.shape.index(max(values.shape))
    spots = []
    for shift in (0, 1):
        where = [jax.random.randint(jax.random.fold_in(key, axis), (), 0, length) for axis, length in enumerate(values.shape)]
        where[longest] = (where[longest] + shift) % values.shape[longest]
        spots.append(tuple(where))
    return values.at[spots[0]].set(least).at[spots[1]].set(largest)


def levels(own_key, shape, shards, low, largest):
    def one(dim, blocks):
        heights = jax.random.uniform(jax.random.fold_in(jax.random.fold_in(own_key, 6), dim), (blocks,), jnp.float32, low / len(shards), largest / len(shards))
        return jnp.repeat(jnp.exp(heights), shape[dim] // blocks).reshape((-1,) + (1,) * (len(shape) - dim - 1))

    loudness = one(*shards[0])
    for cut in shards[1:]:
        loudness = loudness * one(*cut)
    return loudness


def routed_block(stream_key, own, number, rows, amount, top, most, lean):
    ranking = jax.random.permutation(stream_key, amount)
    heavy_load, ordinary = shares(amount, rows * top, most, lean, True), shares(amount, rows * top, most, lean, False)
    places = jnp.arange(amount)

    def named(tallies, turn):
        used = int((tallies > 0).sum())
        fixed = max(1, used // 4)
        shifted = fixed + (places - fixed + turn * (used - fixed)) % max(1, amount - fixed)
        return jnp.zeros((amount,), jnp.int32).at[ranking[jnp.where(places < fixed, places, shifted)]].set(jnp.asarray(tallies, jnp.int32))

    tallies = jnp.where(number % 4 == 0, named(heavy_load, number // 4), named(ordinary, number - number // 4 - 1))
    mixed = jax.random.permutation(jax.random.fold_in(own, 3), amount)
    donor, taker = mixed[0:amount // 2 * 2:2], mixed[1:amount // 2 * 2:2]
    margin = jnp.minimum(tallies[donor] - 1, most - tallies[taker]) // 2
    margin = jnp.where((donor == ranking[0]) | (taker == ranking[0]) | (tallies[taker] == 0), 0, jnp.maximum(margin, 0))
    shifted = jax.random.randint(jax.random.fold_in(own, 4), (amount // 2,), 0, 1 << 20) % (margin + 1)
    tallies = tallies.at[donor].add(-shifted).at[taker].add(shifted)
    labels = jnp.searchsorted(jnp.cumsum(tallies), jnp.arange(rows * top), side="right").astype(jnp.int32)
    table = labels.reshape(top, rows).T
    table = table[jax.random.permutation(jax.random.fold_in(own, 1), rows)]
    turn = jax.random.randint(jax.random.fold_in(own, 2), (rows, 1), 0, top)
    return jnp.take_along_axis(table, (jnp.arange(top)[None, :] + turn) % top, axis=1)


def shares(number_of, total, limit, skew, full):
    portions = [(1 << 20) // math.isqrt(standing ** skew) + 1 for standing in range(1, number_of + 1)]
    largest = limit if full else min(limit, max(-(-total // number_of), total * portions[0] // sum(portions)))
    least = 1 if total - largest >= number_of - 1 else 0
    counts, spare = [largest] + [least] * (number_of - 1), total - largest - least * (number_of - 1)
    while spare > 0:
        movable = [i for i in range(1, number_of) if counts[i] < largest] or [i for i in range(1, number_of) if counts[i] < limit]
        pool, left = sum([portions[i] for i in movable]), spare
        for i in movable:
            addition = min(limit - counts[i], max(1, left * portions[i] // pool), spare)
            counts[i] = counts[i] + addition
            spare = spare - addition
    return np.array(counts)


def centred(key, shape, scale, limit, shards=(), kind=jnp.bfloat16):
    result = scale * jax.random.normal(key, shape, jnp.float32)
    if shards:
        result = result * levels(key, shape, shards, -0.22, 0.18)
    return jnp.clip(result, -limit, limit).astype(kind)


def setup_inputs(seed: int = 0) -> dict:
    splits = jax.random.split(jax.random.key(seed), 7)
    spectra = draw_spectra(jax.random.fold_in(splits[6], 71), 0)
    stacks = centred(splits[1], (STACKS, LAGS), 1.0, 6.0, ((0, 128),), jnp.float32)
    pair_sta = plant(jax.random.randint(splits[2], (2, PAIRS), 0, GSTA), jax.random.fold_in(splits[2], 1), 0, GSTA - 1).astype(jnp.int32)
    pair_valid = plant((jax.random.randint(splits[3], (PAIRS,), 0, 4) < 3).astype(jnp.int32), jax.random.fold_in(splits[3], 1), 0, 1)
    owner_keys = jax.random.split(jax.random.fold_in(splits[4], 1), PAIRS // P_DEV)
    owner_turns = jax.random.permutation(jax.random.fold_in(splits[4], 3), PAIRS // P_DEV)
    owner = jax.vmap(lambda own, number: routed_block(jax.random.fold_in(splits[4], 2), own, number, P_DEV, DEVICES, 1, CAP, 2))(owner_keys, owner_turns).reshape((PAIRS, 1))
    slot = plant(jax.random.randint(splits[5], (PAIRS,), 0, STK_DEV), jax.random.fold_in(splits[5], 1), 0, STK_DEV - 1).astype(jnp.int32)
    return {"spectra": spectra, "stacks": stacks, "pair_sta": pair_sta, "pair_valid": pair_valid, "owner": owner, "slot": slot}


def whiten(spectra):
    shape = spectra.shape
    split = spectra.reshape(shape[0], 2, shape[2] // BAND, BAND)
    power = lax.optimization_barrier(jnp.mean(split * split, axis=(1, 3), keepdims=True))
    return (split * lax.rsqrt(power + 1e-06)).reshape(shape).astype(jnp.bfloat16)

def lag_table():
    freqs = jnp.arange(F, dtype=jnp.int32)
    shifts = jnp.arange(LAGS, dtype=jnp.int32) - (LAGS - 1) // 2
    angle_ids = jnp.mod(freqs[:, None] * shifts[None, :], 2 * F).astype(jnp.int32)
    theta = angle_ids.astype(jnp.float32) * jnp.float32(math.pi / F)
    return jnp.concatenate([jnp.cos(theta), -jnp.sin(theta)], axis=0).astype(jnp.bfloat16)

def reference(spectra, stacks, pair_sta, pair_valid, owner, slot):
    whitened = whiten(spectra)
    table = lag_table()
    groups = (jnp.arange(PAIRS, dtype=jnp.int32) // (P_DEV * N_STA)).astype(jnp.int32)
    first_ids = (groups * GSTA + pair_sta[0]).astype(jnp.int32).reshape(DEVICES, P_DEV)
    second_ids = (groups * GSTA + pair_sta[1]).astype(jnp.int32).reshape(DEVICES, P_DEV)

    def one_block(ids):
        first = whitened[ids[0]].astype(jnp.float32)
        second = whitened[ids[1]].astype(jnp.float32)
        real_part = first[:, 0] * second[:, 0] + first[:, 1] * second[:, 1]
        imag_part = first[:, 1] * second[:, 0] - first[:, 0] * second[:, 1]
        cross = jnp.concatenate([real_part, imag_part], axis=1).astype(jnp.bfloat16)
        return jnp.dot(cross, table, preferred_element_type=jnp.float32)
    corr = lax.map(one_block, (first_ids, second_ids)).reshape(PAIRS, LAGS)
    corr = corr * jnp.float32(F ** (-0.5)) * pair_valid.astype(jnp.float32)[:, None]
    targets = (owner[:, 0] * STK_DEV + slot).astype(jnp.int32)
    return stacks + jnp.zeros_like(stacks).at[targets].add(corr)
```

```python
import functools
import math

import jax
import jax.numpy as jnp
from jax import lax
from jax.experimental import pallas as pl
from jax.experimental.pallas import tpu as pltpu
from jax.sharding import PartitionSpec as P

BAND = 64
MESH = pl.DeviceIdType.MESH
BF16 = jnp.bfloat16
F32 = jnp.float32

BINS = 18432
LAGS = 1601
LAGP = 1664
PAIRS = 96
RING = 8
SLAB = BINS // RING
CHUNKS = 6
CW = SLAB // CHUNKS
MEMBERS = 32
GROUPS = 4
DEVS = 128
STATIONS = 256
SEG = 256
SEGS = 7


def angles(freqs, shifts):
    product = (freqs * shifts).astype(F32)
    turns = jnp.floor(product * F32(1.0 / (2 * BINS)))
    return (product - turns * F32(2 * BINS)) * F32(math.pi / BINS)


def main_kernel(
    x_ref, ids_ref, code_ref, slot_ref, got_ref,
    ws, wr, wc, ids_all, sel, table, acc, cross, a_send, a_recv, b_send, b_recv,
    corr2, gsel, c_send,
    id_send_sem, id_recv_sem, w_send_sem, w_recv_sem,
    a_send_sem, a_recv_sem, b_send_sem, b_recv_sem, c_send_sem, c_recv_sem, own_sem,
):
    grp = lax.axis_index("grp")
    me = lax.axis_index("sta")
    dev = grp * MEMBERS + me
    my_slab = lax.rem(me, RING)
    row = me - my_slab
    my_y = my_slab // 2
    my_c = lax.rem(my_slab, 2)

    barrier = pltpu.get_barrier_semaphore()

    def greet(i, carry):
        peer = lax.rem(dev + i, DEVS)
        pl.semaphore_signal(
            barrier, inc=1,
            device_id={"grp": peer // MEMBERS, "sta": lax.rem(peer, MEMBERS)},
            device_id_type=MESH,
        )
        return carry

    lax.fori_loop(1, DEVS, greet, 0)

    lane = lax.broadcasted_iota(jnp.int32, (128, 128), 1) // BAND
    sub = lax.broadcasted_iota(jnp.int32, (128, 128), 0) // BAND
    bands = jnp.where(lane == sub, F32(1), F32(0))

    def whiten(s, carry):
        base = pl.multiple_of(s * SLAB, 128)
        x0 = x_ref[0, :, pl.ds(base, SLAB)]
        x1 = x_ref[1, :, pl.ds(base, SLAB)]
        square = x0 * x0 + x1 * x1
        tiles = SLAB // 128
        rows = jnp.concatenate([square[:, j * 128 : (j + 1) * 128] for j in range(tiles)], axis=0)
        power = jnp.dot(
            rows, bands, precision=lax.Precision.HIGHEST, preferred_element_type=F32
        ) * F32(1.0 / (2 * BAND))
        inverse = lax.rsqrt(power + F32(1e-06))
        for j in range(tiles):
            inv = inverse[j * 8 : (j + 1) * 8]
            cut = slice(j * 128, (j + 1) * 128)
            both = jnp.concatenate([x0[:, cut] * inv, x1[:, cut] * inv], axis=0).astype(BF16)
            q, o = divmod(j, CW // 128)
            ws[s, q, :, o * 128 : (o + 1) * 128] = both
        return carry

    lax.fori_loop(0, RING, whiten, 0)
    pl.semaphore_wait(barrier, DEVS - 1)

    def send_ids(i, carry):
        peer = row + lax.rem(my_slab + i, RING)
        pltpu.make_async_remote_copy(
            src_ref=ids_ref, dst_ref=ids_all.at[my_slab],
            send_sem=id_send_sem, recv_sem=id_recv_sem,
            device_id={"sta": peer}, device_id_type=MESH,
        ).start()
        return carry

    lax.fori_loop(1, RING, send_ids, 0)
    ids_all[my_slab] = ids_ref[...]

    def send_chunk(q, carry):
        def one(i, inner):
            peer = lax.rem(me + i, MEMBERS)
            pltpu.make_async_remote_copy(
                src_ref=ws.at[lax.rem(peer, RING), q], dst_ref=wr.at[q, me],
                send_sem=w_send_sem.at[q], recv_sem=w_recv_sem.at[q],
                device_id={"sta": peer}, device_id_type=MESH,
            ).start()
            return inner

        lax.fori_loop(1, MEMBERS, one, 0)
        wr[q, me] = ws[my_slab, q]
        return carry

    lax.fori_loop(0, CHUNKS, send_chunk, 0)

    start = my_slab * SLAB

    def table_column(cb, carry):
        lags = lax.broadcasted_iota(jnp.int32, (64, 128), 1) + (cb * 128 - (LAGS - 1) // 2)
        freqs = lax.broadcasted_iota(jnp.int32, (64, 128), 0) + start
        theta = angles(freqs, lags)
        cosines, sines = jnp.cos(theta), jnp.sin(theta)
        turn = angles(jnp.full((8, 128), 64, jnp.int32), lags[:8])
        tc = jnp.concatenate([jnp.cos(turn)] * 8, axis=0)
        ts = jnp.concatenate([jnp.sin(turn)] * 8, axis=0)
        columns = pl.ds(pl.multiple_of(cb * 128, 128), 128)

        def rotate(q, state):
            c, s = state
            for i in range(CW // 64):
                table[q, i * 64 : (i + 1) * 64, columns] = c.astype(BF16)
                table[q, CW + i * 64 : CW + (i + 1) * 64, columns] = (-s).astype(BF16)
                c, s = c * tc - s * ts, s * tc + c * ts
            return c, s

        lax.fori_loop(0, CHUNKS, rotate, (cosines, sines))
        return carry

    lax.fori_loop(0, LAGP // 128, table_column, 0)

    pltpu.make_async_copy(
        ids_all.at[pl.ds(0, RING - 1)], ids_all.at[pl.ds(0, RING - 1)], id_recv_sem
    ).wait()

    def choose(m, carry):
        for side in range(2):
            wanted = ids_all[m, side : side + 1, :]
            station = lax.broadcasted_iota(jnp.int32, (STATIONS, 128), 0)
            hot = jnp.where(station == wanted, F32(1), F32(0))
            sel[side, m] = jnp.transpose(hot)[:PAIRS].astype(BF16)
        return carry

    lax.fori_loop(0, RING, choose, 0)

    def place(t, carry):
        target = lax.broadcasted_iota(jnp.int32, (128, RING * PAIRS), 0) + t * 128
        hot = jnp.where(target == code_ref[0:1, :], F32(1), F32(0)).astype(BF16)
        gsel[pl.ds(pl.multiple_of(t * 128, 128), 128), :] = hot
        return carry

    lax.fori_loop(0, DEVS * 16 // 128, place, 0)

    acc[...] = jnp.zeros_like(acc)

    def chunk(q, carry):
        pltpu.make_async_copy(
            wr.at[q, pl.ds(0, MEMBERS - 1)], wr.at[q, pl.ds(0, MEMBERS - 1)], w_recv_sem.at[q]
        ).wait()

        def repack(i, inner):
            both = wr[q, pl.ds(2 * i, 2)].astype(F32)
            rows = pl.ds(pl.multiple_of(i * 16, 16), 16)
            wc[rows, :CW] = both[:, :8].reshape(16, CW).astype(BF16)
            wc[rows, CW:] = both[:, 8:].reshape(16, CW).astype(BF16)
            return inner

        lax.fori_loop(0, MEMBERS // 2, repack, 0)

        def correlate(m, inner):
            a = jnp.dot(sel[0, m], wc[...], preferred_element_type=F32)
            b = jnp.dot(sel[1, m], wc[...], preferred_element_type=F32)
            a0, a1, b0, b1 = a[:, :CW], a[:, CW:], b[:, :CW], b[:, CW:]
            rows = pl.ds(pl.multiple_of(m * PAIRS, 32), PAIRS)
            cross[rows, :CW] = (a0 * b0 + a1 * b1).astype(BF16)
            cross[rows, CW:] = (a1 * b0 - a0 * b1).astype(BF16)
            return inner

        lax.fori_loop(0, RING, correlate, 0)

        def transform(t, inner):
            columns = pl.ds(pl.multiple_of(t * 256, 256), 256)
            acc[:, columns] += jnp.dot(cross[...], table[q, :, columns], preferred_element_type=F32)
            return inner

        lax.fori_loop(0, LAGP // 256, transform, 0)
        acc[:, LAGP - 128 :] += jnp.dot(
            cross[...], table[q, :, LAGP - 128 :], preferred_element_type=F32
        )
        return carry

    lax.fori_loop(0, CHUNKS, chunk, 0)

    def block(y, c):
        return pl.ds(pl.multiple_of((2 * y + c) * PAIRS, 32), PAIRS)

    a_copies = []
    for i in range(4):
        y = lax.rem(my_y + i + 1, 4)
        a_send[y] = acc[block(y, 1 - my_c), :].astype(BF16)
        copy = pltpu.make_async_remote_copy(
            src_ref=a_send.at[y], dst_ref=a_recv.at[y],
            send_sem=a_send_sem.at[i], recv_sem=a_recv_sem.at[i],
            device_id={"sta": me + 1 - 2 * my_c}, device_id_type=MESH,
        )
        copy.start()
        a_copies.append(copy)
    b_copies = []
    for i in range(3):
        y = lax.rem(my_y + i + 1, 4)
        a_copies[i].wait_recv()
        b_send[i] = (acc[block(y, my_c), :] + a_recv[y].astype(F32)).astype(BF16)
        copy = pltpu.make_async_remote_copy(
            src_ref=b_send.at[i], dst_ref=b_recv.at[i],
            send_sem=b_send_sem.at[i], recv_sem=b_recv_sem.at[i],
            device_id={"sta": row + 2 * y + my_c}, device_id_type=MESH,
        )
        copy.start()
        b_copies.append(copy)
    a_copies[3].wait_recv()
    mine = block(my_y, my_c)
    acc[mine, :] = acc[mine, :] + a_recv[my_y].astype(F32)
    for copy in b_copies:
        copy.wait_recv()
    scale = F32(BINS ** (-0.5))
    for k in range(SEGS):
        width = min(SEG, LAGP - k * SEG)
        cut = slice(k * SEG, k * SEG + width)
        total = acc[mine, cut]
        for i in range(3):
            total = total + b_recv[i, :, cut].astype(F32)
        corr2[k * PAIRS : (k + 1) * PAIRS, :width] = (total * scale).astype(BF16)
        if width < SEG:
            corr2[k * PAIRS : (k + 1) * PAIRS, width:] = jnp.zeros((PAIRS, SEG - width), BF16)
    corr2[SEGS * PAIRS :, :] = slot_ref[...]

    def pack(t, carry):
        rows = pl.ds(pl.multiple_of(t * 256, 256), 256)
        out = jnp.dot(gsel[rows, :], corr2[...], preferred_element_type=F32)
        c_send[pl.ds(t * 16, 16)] = out.reshape(16, 16, SEG).astype(BF16)
        return carry

    lax.fori_loop(0, DEVS // 16, pack, 0)
    own = pltpu.make_async_copy(c_send.at[dev], got_ref.at[dev], own_sem)
    own.start()

    def route(i, carry):
        peer = lax.rem(dev + i, DEVS)
        pltpu.make_async_remote_copy(
            src_ref=c_send.at[peer], dst_ref=got_ref.at[dev],
            send_sem=c_send_sem, recv_sem=c_recv_sem,
            device_id={"grp": peer // MEMBERS, "sta": lax.rem(peer, MEMBERS)},
            device_id_type=MESH,
        ).start()
        return carry

    lax.fori_loop(1, DEVS, route, 0)

    for i in range(4):
        a_copies[i].wait_send()
    for i in range(3):
        b_copies[i].wait_send()
    pltpu.make_async_copy(
        ids_all.at[pl.ds(0, RING - 1)], ids_all.at[pl.ds(0, RING - 1)], id_send_sem
    ).wait()

    def sent(q, carry):
        pltpu.make_async_copy(
            wr.at[q, pl.ds(0, MEMBERS - 1)], wr.at[q, pl.ds(0, MEMBERS - 1)], w_send_sem.at[q]
        ).wait()
        return carry

    lax.fori_loop(0, CHUNKS, sent, 0)
    own.wait()
    rest = c_send.at[pl.ds(0, DEVS - 1)]
    pltpu.make_async_copy(rest, rest, c_send_sem).wait()
    pltpu.make_async_copy(rest, rest, c_recv_sem).wait()


def correlate_and_route(x, ids, code, slots):
    vmem = pl.BlockSpec(memory_space=pltpu.VMEM)
    dma = pltpu.SemaphoreType.DMA
    return pl.pallas_call(
        main_kernel,
        out_shape=jax.ShapeDtypeStruct((DEVS, 16, SEG), BF16),
        in_specs=[vmem] * 4,
        out_specs=pl.BlockSpec(memory_space=pl.ANY),
        scratch_shapes=[
            pltpu.VMEM((RING, CHUNKS, 16, CW), BF16),
            pltpu.VMEM((CHUNKS, MEMBERS, 16, CW), BF16),
            pltpu.VMEM((STATIONS, 2 * CW), BF16),
            pltpu.VMEM((RING, 8, 128), jnp.int32),
            pltpu.VMEM((2, RING, PAIRS, STATIONS), BF16),
            pltpu.VMEM((CHUNKS, 2 * CW, LAGP), BF16),
            pltpu.VMEM((RING * PAIRS, LAGP), F32),
            pltpu.VMEM((RING * PAIRS, 2 * CW), BF16),
            pltpu.VMEM((4, PAIRS, LAGP), BF16),
            pltpu.VMEM((4, PAIRS, LAGP), BF16),
            pltpu.VMEM((3, PAIRS, LAGP), BF16),
            pltpu.VMEM((3, PAIRS, LAGP), BF16),
            pltpu.VMEM((RING * PAIRS, SEG), BF16),
            pltpu.VMEM((DEVS * 16, RING * PAIRS), BF16),
            pltpu.VMEM((DEVS, 16, SEG), BF16),
            dma, dma,
            dma((CHUNKS,)), dma((CHUNKS,)),
            dma((4,)), dma((4,)),
            dma((3,)), dma((3,)),
            dma, dma, dma,
        ],
        compiler_params=pltpu.CompilerParams(
            collective_id=0, has_side_effects=True, vmem_limit_bytes=60 * 1024 * 1024
        ),
    )(x, ids, code, slots)


def stack_kernel(got_ref, stacks_ref, out_ref):
    rows = DEVS * 16
    got = got_ref[...].reshape(rows, SEG)
    first = jnp.where(lax.broadcasted_iota(jnp.int32, (8, SEG), 1) == 0, F32(1), F32(0)).astype(BF16)
    marks = lax.dot_general(first, got, (((1,), (1,)), ((), ())), preferred_element_type=F32)
    place = lax.broadcasted_iota(jnp.int32, (8, rows), 1) & 15

    def spread(values, offset):
        def back(v, n):
            return pltpu.roll(v, rows - n, 1)

        values = back(values, offset)
        values = jnp.maximum(values, back(values, 1))
        values = jnp.maximum(values, back(values, 2))
        return jnp.maximum(values, back(values, 3))

    slots = jnp.maximum(
        spread(jnp.where(place == 14, marks, F32(0)), 8),
        spread(jnp.where(place == 15, marks, F32(0)), 2),
    )
    segment = jnp.where(place < 7, place, place - 7)
    code = jnp.where(place < 14, slots.astype(jnp.int32) + segment * PAIRS, -1)[0:1]
    for k in range(SEGS):
        want = lax.broadcasted_iota(jnp.int32, (PAIRS, rows), 0) + k * PAIRS
        hot = jnp.where(want == code, F32(1), F32(0)).astype(BF16)
        part = jnp.dot(hot, got, preferred_element_type=F32)
        width = min(SEG, LAGS - k * SEG)
        cut = slice(k * SEG, k * SEG + width)
        out_ref[:, cut] = stacks_ref[:, cut] + part[:, :width]


def add_rows(got, stacks):
    vmem = pl.BlockSpec(memory_space=pltpu.VMEM)
    return pl.pallas_call(
        stack_kernel,
        out_shape=jax.ShapeDtypeStruct(stacks.shape, F32),
        in_specs=[vmem] * 2,
        out_specs=vmem,
        compiler_params=pltpu.CompilerParams(vmem_limit_bytes=40 * 1024 * 1024),
    )(got, stacks)


def local(spectra, stacks, pair_sta, pair_valid, owner, slot):
    x = jnp.transpose(spectra, (1, 0, 2))
    ids = jnp.pad(pair_sta, ((0, 6), (0, 128 - PAIRS)))
    dest = owner[:, 0]
    order = lax.iota(jnp.int32, PAIRS)
    same = (dest[:, None] == dest[None, :]) & (order[:, None] < order[None, :])
    position = jnp.sum(same.astype(jnp.int32), axis=0)
    base = dest * 16
    code = (base + position * 7)[None, :] + lax.iota(jnp.int32, SEGS)[:, None]
    code = jnp.where(pair_valid[None, :] == 1, code, -1)
    code = jnp.concatenate([code, (base + 14 + position)[None, :]], axis=0).reshape(1, RING * PAIRS)
    code = jnp.broadcast_to(code, (8, RING * PAIRS))
    slots = jnp.broadcast_to(slot.astype(BF16)[:, None], (PAIRS, SEG))
    got = correlate_and_route(x, ids, code, slots)
    return add_rows(got, stacks)


def solution(mesh):
    return jax.shard_map(
        local,
        mesh=mesh,
        in_specs=(
            P(("grp", "sta"), None, None),
            P(("grp", "sta"), None),
            P(None, ("grp", "sta")),
            P(("grp", "sta")),
            P(("grp", "sta"), None),
            P(("grp", "sta")),
        ),
        out_specs=P(("grp", "sta"), None),
        check_vma=False,
    )
```

```python
import functools
import math

import jax
import jax.numpy as jnp
from jax import lax
from jax.experimental import pallas as pl
from jax.experimental.pallas import tpu as pltpu
from jax.sharding import PartitionSpec as P

BAND = 64
MESH = pl.DeviceIdType.MESH
BF16 = jnp.bfloat16
F32 = jnp.float32

BINS = 18432
LAGS = 1601
HALF = (LAGS + 1) // 2
SIDE = 832
COLS = 2 * SIDE
PAIRS = 96
RING = 8
SLAB = BINS // RING
WIDTHS = (768, 768, 512, 256)
STARTS = (0, 768, 1536, 2048)
PARTS = len(WIDTHS)
MEMBERS = 32
GROUPS = 4
DEVS = 128
STATIONS = 256
SEG = 256
SEGS = 7


def angles(freqs, shifts):
    product = (freqs * shifts).astype(F32)
    turns = jnp.floor(product * F32(1.0 / (2 * BINS)))
    return (product - turns * F32(2 * BINS)) * F32(math.pi / BINS)


def main_kernel(x_ref, meta_ref, got_ref, *scratch):
    ws, wr = scratch[:PARTS], scratch[PARTS : 2 * PARTS]
    (
        wc, ids_all, sel, tcos, tsin, acc, cross, a_send, a_recv, b_send, b_recv,
        corr2, gsel, c_send,
        id_send_sem, id_recv_sem, w_send_sem, w_recv_sem,
        a_send_sem, a_recv_sem, b_send_sem, b_recv_sem, c_send_sem, c_recv_sem, own_sem,
    ) = scratch[2 * PARTS :]
    grp = lax.axis_index("grp")
    me = lax.axis_index("sta")
    dev = grp * MEMBERS + me
    my_slab = lax.rem(me, RING)
    row = me - my_slab
    my_y = my_slab // 2
    my_c = lax.rem(my_slab, 2)

    barrier = pltpu.get_barrier_semaphore()

    def greet(i, carry):
        peer = lax.rem(dev + i, DEVS)
        pl.semaphore_signal(
            barrier, inc=1,
            device_id={"grp": peer // MEMBERS, "sta": lax.rem(peer, MEMBERS)},
            device_id_type=MESH,
        )
        return carry

    lax.fori_loop(1, DEVS, greet, 0)

    lane = lax.broadcasted_iota(jnp.int32, (128, 128), 1) // BAND
    sub = lax.broadcasted_iota(jnp.int32, (128, 128), 0) // BAND
    bands = jnp.where(lane == sub, F32(1), F32(0))

    def whiten(s, carry):
        base = pl.multiple_of(s * SLAB, 128)
        x0 = x_ref[:, 0, pl.ds(base, SLAB)]
        x1 = x_ref[:, 1, pl.ds(base, SLAB)]
        square = x0 * x0 + x1 * x1
        tiles = SLAB // 128
        rows = jnp.concatenate([square[:, j * 128 : (j + 1) * 128] for j in range(tiles)], axis=0)
        power = jnp.dot(
            rows, bands, precision=lax.Precision.HIGHEST, preferred_element_type=F32
        ) * F32(1.0 / (2 * BAND))
        inverse = lax.rsqrt(power + F32(1e-06))
        for j in range(tiles):
            inv = inverse[j * 8 : (j + 1) * 8]
            cut = slice(j * 128, (j + 1) * 128)
            both = jnp.concatenate([x0[:, cut] * inv, x1[:, cut] * inv], axis=0).astype(BF16)
            q = max(p for p in range(PARTS) if STARTS[p] <= j * 128)
            o = j * 128 - STARTS[q]
            ws[q][s, :, o : o + 128] = both
        return carry

    lax.fori_loop(0, RING, whiten, 0)
    pl.semaphore_wait(barrier, DEVS - 1)

    def send_ids(i, carry):
        peer = row + lax.rem(my_slab + i, RING)
        pltpu.make_async_remote_copy(
            src_ref=meta_ref, dst_ref=ids_all.at[my_slab],
            send_sem=id_send_sem, recv_sem=id_recv_sem,
            device_id={"sta": peer}, device_id_type=MESH,
        ).start()
        return carry

    lax.fori_loop(1, RING, send_ids, 0)
    ids_all[my_slab] = meta_ref[...]

    def send_part(q):
        def one(i, carry):
            peer = lax.rem(me + i, MEMBERS)
            pltpu.make_async_remote_copy(
                src_ref=ws[q].at[lax.rem(peer, RING)], dst_ref=wr[q].at[me],
                send_sem=w_send_sem.at[q], recv_sem=w_recv_sem.at[q],
                device_id={"sta": peer}, device_id_type=MESH,
            ).start()
            return carry

        lax.fori_loop(1, MEMBERS, one, 0)
        wr[q][me] = ws[q][my_slab]

    for q in range(PARTS):
        send_part(q)

    start = my_slab * SLAB

    def table_column(cb, half):
        column = lax.broadcasted_iota(jnp.int32, (64, 128), 1) + cb * 128
        cosine_side = column < SIDE
        lags = jnp.where(cosine_side, column, column - SIDE)
        freqs = lax.broadcasted_iota(jnp.int32, (64, 128), 0) + start
        theta = angles(freqs, lags)
        cosines, sines = jnp.cos(theta), jnp.sin(theta)
        turn = angles(jnp.full((8, 128), 64, jnp.int32), lags[:8])
        tc = jnp.concatenate([jnp.cos(turn)] * 8, axis=0)
        ts = jnp.concatenate([jnp.sin(turn)] * 8, axis=0)

        def rotate(i, state):
            c, s = state
            for step in range(4):
                rows = pl.ds(pl.multiple_of(i * 256 + step * 64, 64), 64)
                if half == "both":
                    tcos[rows, SIDE - 64 : SIDE + 64] = jnp.where(cosine_side, c, F32(0)).astype(BF16)
                    tsin[rows, :128] = jnp.where(cosine_side, F32(0), -s).astype(BF16)
                elif half == "cos":
                    tcos[rows, pl.ds(pl.multiple_of(cb * 128, 128), 128)] = c.astype(BF16)
                else:
                    tsin[rows, pl.ds(pl.multiple_of(cb * 128 - 768, 128), 128)] = (-s).astype(BF16)
                c, s = c * tc - s * ts, s * tc + c * ts
            return c, s

        lax.fori_loop(0, SLAB // 256, rotate, (cosines, sines))

    def cosine_column(cb, carry):
        table_column(cb, "cos")
        return carry

    def sine_column(cb, carry):
        table_column(cb, "sin")
        return carry

    lax.fori_loop(0, 6, cosine_column, 0)
    table_column(6, "both")
    lax.fori_loop(7, 13, sine_column, 0)

    pltpu.make_async_copy(
        ids_all.at[pl.ds(0, RING - 1)], ids_all.at[pl.ds(0, RING - 1)], id_recv_sem
    ).wait()

    def choose(m, carry):
        station = lax.broadcasted_iota(jnp.int32, (STATIONS, 128), 0)
        for side in range(2):
            wanted = ids_all[m, side : side + 1, :]
            hot = jnp.transpose(jnp.where(station == wanted, F32(1), F32(0))).astype(BF16)
            for i in range(PAIRS // 16):
                sel[m, i * 32 + side * 16 : i * 32 + side * 16 + 16, :] = hot[i * 16 : (i + 1) * 16]
        return carry

    lax.fori_loop(0, RING, choose, 0)

    for q in range(PARTS):
        width = WIDTHS[q]
        arrived = wr[q].at[pl.ds(0, MEMBERS - 1)]
        pltpu.make_async_copy(arrived, arrived, w_recv_sem.at[q]).wait()

        def repack(i, carry):
            both = wr[q][pl.ds(2 * i, 2)].astype(F32)
            rows = pl.ds(pl.multiple_of(i * 16, 16), 16)
            low = both[:, :8].reshape(16, width).astype(BF16)
            high = both[:, 8:].reshape(16, width).astype(BF16)
            for j in range(width // 128):
                wc[j, rows, :128] = low[:, j * 128 : (j + 1) * 128]
                wc[j, rows, 128:] = high[:, j * 128 : (j + 1) * 128]
            return carry

        lax.fori_loop(0, MEMBERS // 2, repack, 0)

        def correlate(j, carry):
            real_at = pl.ds(pl.multiple_of(j * 128, 128), 128)
            imag_at = pl.ds(pl.multiple_of(768 + j * 128, 128), 128)
            for m in range(0, RING, 4):
                both = jnp.dot(
                    sel[m : m + 4].reshape(4 * 2 * PAIRS, STATIONS), wc[j], preferred_element_type=F32
                )
                for i in range(4 * PAIRS // 16):
                    a0, a1 = both[i * 32 : i * 32 + 16, :128], both[i * 32 : i * 32 + 16, 128:]
                    b0, b1 = both[i * 32 + 16 : i * 32 + 32, :128], both[i * 32 + 16 : i * 32 + 32, 128:]
                    rows = slice(m * PAIRS + i * 16, m * PAIRS + i * 16 + 16)
                    cross[rows, real_at] = (a0 * b0 + a1 * b1).astype(BF16)
                    cross[rows, imag_at] = (a1 * b0 - a0 * b1).astype(BF16)
            return carry

        lax.fori_loop(0, width // 128, correlate, 0)

        bins = slice(STARTS[q], STARTS[q] + width)

        def add(columns, value):
            if q == 0:
                acc[:, columns] = value
            else:
                acc[:, columns] += value

        def transform(t, carry):
            left = pl.ds(pl.multiple_of(t * 256, 256), 256)
            right = pl.ds(pl.multiple_of(t * 256 + 128, 128), 256)
            far = pl.ds(pl.multiple_of(t * 256 + 896, 128), 256)
            add(left, jnp.dot(cross[:, :width], tcos[bins, left], preferred_element_type=F32))
            add(far, jnp.dot(cross[:, 768 : 768 + width], tsin[bins, right], preferred_element_type=F32))
            return carry

        lax.fori_loop(0, 3, transform, 0)
        add(
            slice(768, 896),
            jnp.dot(cross[:, :width], tcos[bins, 768:], preferred_element_type=F32)
            + jnp.dot(cross[:, 768 : 768 + width], tsin[bins, :128], preferred_element_type=F32),
        )

    def block(y, c):
        return pl.ds(pl.multiple_of((2 * y + c) * PAIRS, 32), PAIRS)

    a_copies = []
    for i in range(4):
        y = lax.rem(my_y + i + 1, 4)
        a_send[y] = acc[block(y, 1 - my_c), :].astype(BF16)
        copy = pltpu.make_async_remote_copy(
            src_ref=a_send.at[y], dst_ref=a_recv.at[y],
            send_sem=a_send_sem.at[i], recv_sem=a_recv_sem.at[i],
            device_id={"sta": me + 1 - 2 * my_c}, device_id_type=MESH,
        )
        copy.start()
        a_copies.append(copy)
    meta = meta_ref[...]
    square = (128, 128)
    sub, lane = lax.broadcasted_iota(jnp.int32, square, 0), lax.broadcasted_iota(jnp.int32, square, 1)
    dest = meta[3:4, :]
    dest_across = jnp.transpose(jnp.broadcast_to(dest.astype(F32), square)).astype(jnp.int32)
    earlier = (dest_across == dest) & (sub < lane) & (sub < PAIRS)
    position = jnp.sum(jnp.where(earlier, F32(1), F32(0)), axis=0, keepdims=True).astype(jnp.int32)
    real_pair = lane[0:1] < PAIRS
    counted = real_pair & (meta[2:3, :] == 1)
    row_code = jnp.where(counted, dest * 16 + position * SEGS, -64)
    slot_code = jnp.where(real_pair, dest * 16 + 2 * SEGS + position, -64)

    def place(t, carry):
        target = lax.broadcasted_iota(jnp.int32, (128, 128), 0) + t * 128
        rows = pl.ds(pl.multiple_of(t * 128, 128), 128)
        for k in range(SEGS + 1):
            code = slot_code if k == SEGS else row_code + k
            gsel[rows, k * 128 : (k + 1) * 128] = jnp.where(target == code, F32(1), F32(0)).astype(BF16)
        return carry

    lax.fori_loop(0, DEVS * 16 // 128, place, 0)
    slot_across = jnp.transpose(jnp.broadcast_to(meta[4:5, :].astype(F32), square)).astype(BF16)
    corr2[SEGS * 128 :, :128] = slot_across
    corr2[SEGS * 128 :, 128:] = slot_across

    b_copies = []
    for i in range(3):
        y = lax.rem(my_y + i + 1, 4)
        a_copies[i].wait_recv()
        b_send[i] = (acc[block(y, my_c), :] + a_recv[y].astype(F32)).astype(BF16)
        copy = pltpu.make_async_remote_copy(
            src_ref=b_send.at[i], dst_ref=b_recv.at[i],
            send_sem=b_send_sem.at[i], recv_sem=b_recv_sem.at[i],
            device_id={"sta": row + 2 * y + my_c}, device_id_type=MESH,
        )
        copy.start()
        b_copies.append(copy)
    a_copies[3].wait_recv()
    mine = block(my_y, my_c)
    acc[mine, :] = acc[mine, :] + a_recv[my_y].astype(F32)
    for copy in b_copies:
        copy.wait_recv()
    scale = F32(BINS ** (-0.5))
    for k in range(SEGS):
        width = min(SEG, COLS - k * SEG)
        cut = slice(k * SEG, k * SEG + width)
        total = acc[mine, cut]
        for i in range(3):
            total = total + b_recv[i, :, cut].astype(F32)
        corr2[k * 128 : k * 128 + PAIRS, :width] = (total * scale).astype(BF16)
        corr2[k * 128 + PAIRS : (k + 1) * 128, :] = jnp.zeros((128 - PAIRS, SEG), BF16)
        if width < SEG:
            corr2[k * 128 : k * 128 + PAIRS, width:] = jnp.zeros((PAIRS, SEG - width), BF16)

    def pack(t, carry):
        rows = pl.ds(pl.multiple_of(t * 256, 256), 256)
        out = jnp.dot(gsel[rows, :], corr2[...], preferred_element_type=F32)
        c_send[pl.ds(t * 16, 16)] = out.reshape(16, 16, SEG).astype(BF16)
        return carry

    lax.fori_loop(0, DEVS // 16, pack, 0)
    own = pltpu.make_async_copy(c_send.at[dev], got_ref.at[dev], own_sem)
    own.start()

    def route(i, carry):
        peer = lax.rem(dev + i, DEVS)
        pltpu.make_async_remote_copy(
            src_ref=c_send.at[peer], dst_ref=got_ref.at[dev],
            send_sem=c_send_sem, recv_sem=c_recv_sem,
            device_id={"grp": peer // MEMBERS, "sta": lax.rem(peer, MEMBERS)},
            device_id_type=MESH,
        ).start()
        return carry

    lax.fori_loop(1, DEVS, route, 0)

    for i in range(4):
        a_copies[i].wait_send()
    for i in range(3):
        b_copies[i].wait_send()
    pltpu.make_async_copy(
        ids_all.at[pl.ds(0, RING - 1)], ids_all.at[pl.ds(0, RING - 1)], id_send_sem
    ).wait()

    for q in range(PARTS):
        sent = wr[q].at[pl.ds(0, MEMBERS - 1)]
        pltpu.make_async_copy(sent, sent, w_send_sem.at[q]).wait()
    own.wait()
    rest = c_send.at[pl.ds(0, DEVS - 1)]
    pltpu.make_async_copy(rest, rest, c_send_sem).wait()
    pltpu.make_async_copy(rest, rest, c_recv_sem).wait()


def correlate_and_route(x, meta):
    vmem = pl.BlockSpec(memory_space=pltpu.VMEM)
    dma = pltpu.SemaphoreType.DMA
    return pl.pallas_call(
        main_kernel,
        out_shape=jax.ShapeDtypeStruct((DEVS, 16, SEG), BF16),
        in_specs=[vmem] * 2,
        out_specs=pl.BlockSpec(memory_space=pl.ANY),
        scratch_shapes=[
            *[pltpu.VMEM((RING, 16, w), BF16) for w in WIDTHS],
            *[pltpu.VMEM((MEMBERS, 16, w), BF16) for w in WIDTHS],
            pltpu.VMEM((max(WIDTHS) // 128, STATIONS, 256), BF16),
            pltpu.VMEM((RING, 8, 128), jnp.int32),
            pltpu.VMEM((RING, 2 * PAIRS, STATIONS), BF16),
            pltpu.VMEM((SLAB, 896), BF16),
            pltpu.VMEM((SLAB, 896), BF16),
            pltpu.VMEM((RING * PAIRS, COLS), F32),
            pltpu.VMEM((RING * PAIRS, 2 * max(WIDTHS)), BF16),
            pltpu.VMEM((4, PAIRS, COLS), BF16),
            pltpu.VMEM((4, PAIRS, COLS), BF16),
            pltpu.VMEM((3, PAIRS, COLS), BF16),
            pltpu.VMEM((3, PAIRS, COLS), BF16),
            pltpu.VMEM(((SEGS + 1) * 128, SEG), BF16),
            pltpu.VMEM((DEVS * 16, (SEGS + 1) * 128), BF16),
            pltpu.VMEM((DEVS, 16, SEG), BF16),
            dma, dma,
            dma((PARTS,)), dma((PARTS,)),
            dma((4,)), dma((4,)),
            dma((3,)), dma((3,)),
            dma, dma, dma,
        ],
        compiler_params=pltpu.CompilerParams(
            collective_id=0, has_side_effects=True, vmem_limit_bytes=46 * 1024 * 1024
        ),
    )(x, meta)


def stack_kernel(got_ref, stacks_ref, out_ref):
    rows = DEVS * 16
    got = got_ref[...].reshape(rows, SEG)
    first = jnp.where(lax.broadcasted_iota(jnp.int32, (8, SEG), 1) == 0, F32(1), F32(0)).astype(BF16)
    marks = lax.dot_general(first, got, (((1,), (1,)), ((), ())), preferred_element_type=F32)
    place = lax.broadcasted_iota(jnp.int32, (8, rows), 1) & 15

    def spread(values, offset):
        def back(v, n):
            return pltpu.roll(v, rows - n, 1)

        values = back(values, offset)
        values = jnp.maximum(values, back(values, 1))
        values = jnp.maximum(values, back(values, 2))
        return jnp.maximum(values, back(values, 3))

    slots = jnp.maximum(
        spread(jnp.where(place == 14, marks, F32(0)), 8),
        spread(jnp.where(place == 15, marks, F32(0)), 2),
    )
    segment = jnp.where(place < 7, place, place - 7)
    code = jnp.where(place < 14, slots.astype(jnp.int32) + segment * PAIRS, -1)[0:1]
    parts = []
    for k in range(SEGS):
        want = lax.broadcasted_iota(jnp.int32, (PAIRS, rows), 0) + k * PAIRS
        hot = jnp.where(want == code, F32(1), F32(0)).astype(BF16)
        parts.append(jnp.dot(hot, got, preferred_element_type=F32))
    sums = jnp.concatenate(parts, axis=1)
    even, odd = sums[:, :896], sums[:, SIDE : SIDE + 896]
    tiles = 7
    gap = even - odd
    high = gap.astype(BF16)
    low = (gap - high.astype(F32)).astype(BF16)
    stack = jnp.concatenate(
        [v[:, t * 128 : (t + 1) * 128] for v in (high, low) for t in range(tiles)], axis=0
    )
    mirror = lax.broadcasted_iota(jnp.int32, (128, 128), 0) + lax.broadcasted_iota(jnp.int32, (128, 128), 1)
    mirror = jnp.where(mirror == 127, F32(1), F32(0)).astype(BF16)
    turned = jnp.dot(stack, mirror, preferred_element_type=F32)
    turned = turned[: tiles * PAIRS] + turned[tiles * PAIRS :]
    behind = jnp.concatenate(
        [turned[t * PAIRS : (t + 1) * PAIRS] for t in reversed(range(tiles))], axis=1
    )
    skip = tiles * 128 - HALF
    out_ref[:, :HALF] = stacks_ref[:, :HALF] + behind[:, skip:]
    out_ref[:, HALF:] = stacks_ref[:, HALF:] + (even + odd)[:, 1:HALF]


def add_rows(got, stacks):
    vmem = pl.BlockSpec(memory_space=pltpu.VMEM)
    return pl.pallas_call(
        stack_kernel,
        out_shape=jax.ShapeDtypeStruct(stacks.shape, F32),
        in_specs=[vmem] * 2,
        out_specs=vmem,
        compiler_params=pltpu.CompilerParams(vmem_limit_bytes=40 * 1024 * 1024),
    )(got, stacks)


def local(spectra, stacks, pair_sta, pair_valid, owner, slot):
    rows = [pair_sta, pair_valid[None, :], owner.reshape(1, PAIRS), slot[None, :]]
    meta = jnp.pad(jnp.concatenate(rows, axis=0), ((0, 3), (0, 128 - PAIRS)))
    got = correlate_and_route(spectra, meta)
    return add_rows(got, stacks)


def solution(mesh):
    return jax.shard_map(
        local,
        mesh=mesh,
        in_specs=(
            P(("grp", "sta"), None, None),
            P(("grp", "sta"), None),
            P(None, ("grp", "sta")),
            P(("grp", "sta")),
            P(("grp", "sta"), None),
            P(("grp", "sta")),
        ),
        out_specs=P(("grp", "sta"), None),
        check_vma=False,
    )
```

```python
import functools
import math

import jax
import jax.numpy as jnp
from jax import lax
from jax.experimental import pallas as pl
from jax.experimental.pallas import tpu as pltpu
from jax.sharding import PartitionSpec as P

BAND = 64
MESH = pl.DeviceIdType.MESH
BF16 = jnp.bfloat16
F32 = jnp.float32

BINS = 18432
LAGS = 1601
HALF = (LAGS + 1) // 2
SIDE = 832
COLS = 2 * SIDE
PAIRS = 96
SHARE = PAIRS // 2
RING = 8
BLOCKS = 2 * RING
SLAB = BINS // RING
WIDTHS = (768, 768, 512, 256)
STARTS = (0, 768, 1536, 2048)
PARTS = len(WIDTHS)
MEMBERS = 32
GROUPS = 4
DEVS = 128
STATIONS = 256
SEG = 256
SEGS = 4
PIECES = ((0, 1024), (1024, 640))


def angles(freqs, shifts):
    product = (freqs * shifts).astype(F32)
    turns = jnp.floor(product * F32(1.0 / (2 * BINS)))
    return (product - turns * F32(2 * BINS)) * F32(math.pi / BINS)


def main_kernel(x_ref, meta_ref, got_a, got_b, *scratch):
    ws, wr = scratch[:PARTS], scratch[PARTS : 2 * PARTS]
    (
        wc, ids_all, sel, tcos, tsin, acc, cross,
        a_send_0, a_send_1, a_recv_0, a_recv_1, b_send_0, b_send_1, b_recv_0, b_recv_1,
        corr_0, corr_1, gsel, c_send_0, c_send_1,
        id_send_sem, id_recv_sem, w_send_sem, w_recv_sem,
        a_send_sem, a_recv_sem, b_send_sem, b_recv_sem, c_send_sem, c_recv_sem, own_sem,
    ) = scratch[2 * PARTS :]
    a_send, a_recv = (a_send_0, a_send_1), (a_recv_0, a_recv_1)
    b_send, b_recv = (b_send_0, b_send_1), (b_recv_0, b_recv_1)
    corr, c_send, got = (corr_0, corr_1), (c_send_0, c_send_1), (got_a, got_b)
    grp = lax.axis_index("grp")
    me = lax.axis_index("sta")
    dev = grp * MEMBERS + me
    my_z, inside = me // RING, lax.rem(me, RING)
    my_y, my_c = inside // 2, lax.rem(inside, 2)

    def slab_of(member):
        z, rest = member // RING, lax.rem(member, RING)
        return 2 * lax.rem(z + rest // 2, 4) + lax.rem(rest, 2)

    my_slab = slab_of(me)
    row = me - inside

    barrier = pltpu.get_barrier_semaphore()

    def greet(i, carry):
        peer = lax.rem(dev + i, DEVS)
        pl.semaphore_signal(
            barrier, inc=1,
            device_id={"grp": peer // MEMBERS, "sta": lax.rem(peer, MEMBERS)},
            device_id_type=MESH,
        )
        return carry

    lax.fori_loop(1, DEVS, greet, 0)

    lane = lax.broadcasted_iota(jnp.int32, (128, 128), 1) // BAND
    sub = lax.broadcasted_iota(jnp.int32, (128, 128), 0) // BAND
    bands = jnp.where(lane == sub, F32(1), F32(0))

    def whiten(s, carry):
        base = pl.multiple_of(s * SLAB, 128)
        x0 = x_ref[:, 0, pl.ds(base, SLAB)]
        x1 = x_ref[:, 1, pl.ds(base, SLAB)]
        square = x0 * x0 + x1 * x1
        tiles = SLAB // 128
        rows = jnp.concatenate([square[:, j * 128 : (j + 1) * 128] for j in range(tiles)], axis=0)
        power = jnp.dot(
            rows, bands, precision=lax.Precision.HIGHEST, preferred_element_type=F32
        ) * F32(1.0 / (2 * BAND))
        inverse = lax.rsqrt(power + F32(1e-06))
        for j in range(tiles):
            inv = inverse[j * 8 : (j + 1) * 8]
            cut = slice(j * 128, (j + 1) * 128)
            both = jnp.concatenate([x0[:, cut] * inv, x1[:, cut] * inv], axis=0).astype(BF16)
            q = max(p for p in range(PARTS) if STARTS[p] <= j * 128)
            o = j * 128 - STARTS[q]
            ws[q][s, :, o : o + 128] = both
        return carry

    lax.fori_loop(0, RING, whiten, 0)
    pl.semaphore_wait(barrier, DEVS - 1)

    def send_ids(slot, peer):
        pltpu.make_async_remote_copy(
            src_ref=meta_ref, dst_ref=ids_all.at[slot],
            send_sem=id_send_sem, recv_sem=id_recv_sem,
            device_id={"sta": peer}, device_id_type=MESH,
        ).start()

    def along_y(i, carry):
        send_ids(inside, row + lax.rem(inside + i, RING))
        return carry

    def along_z(i, carry):
        send_ids(RING + 2 * my_z + my_c, lax.rem(my_z + 1 + i // 2, 4) * RING + 2 * my_y + lax.rem(i, 2))
        return carry

    lax.fori_loop(1, RING, along_y, 0)
    lax.fori_loop(0, 6, along_z, 0)
    ids_all[inside] = meta_ref[...]
    ids_all[RING + 2 * my_z + my_c] = meta_ref[...]

    def send_part(q):
        def one(i, carry):
            peer = lax.rem(me + i * 11, MEMBERS)
            pltpu.make_async_remote_copy(
                src_ref=ws[q].at[slab_of(peer)], dst_ref=wr[q].at[me],
                send_sem=w_send_sem.at[q], recv_sem=w_recv_sem.at[q],
                device_id={"sta": peer}, device_id_type=MESH,
            ).start()
            return carry

        lax.fori_loop(1, MEMBERS, one, 0)
        wr[q][me] = ws[q][my_slab]

    for q in range(PARTS):
        send_part(q)

    start = my_slab * SLAB

    def table_column(cb, half):
        column = lax.broadcasted_iota(jnp.int32, (64, 128), 1) + cb * 128
        cosine_side = column < SIDE
        lags = jnp.where(cosine_side, column, column - SIDE)
        freqs = lax.broadcasted_iota(jnp.int32, (64, 128), 0) + start
        theta = angles(freqs, lags)
        cosines, sines = jnp.cos(theta), jnp.sin(theta)
        turn = angles(jnp.full((8, 128), 64, jnp.int32), lags[:8])
        tc = jnp.concatenate([jnp.cos(turn)] * 8, axis=0)
        ts = jnp.concatenate([jnp.sin(turn)] * 8, axis=0)

        def rotate(i, state):
            c, s = state
            for step in range(4):
                rows = pl.ds(pl.multiple_of(i * 256 + step * 64, 64), 64)
                if half == "both":
                    tcos[rows, SIDE - 64 : SIDE + 64] = jnp.where(cosine_side, c, F32(0)).astype(BF16)
                    tsin[rows, :128] = jnp.where(cosine_side, F32(0), -s).astype(BF16)
                elif half == "cos":
                    tcos[rows, pl.ds(pl.multiple_of(cb * 128, 128), 128)] = c.astype(BF16)
                else:
                    tsin[rows, pl.ds(pl.multiple_of(cb * 128 - 768, 128), 128)] = (-s).astype(BF16)
                c, s = c * tc - s * ts, s * tc + c * ts
            return c, s

        lax.fori_loop(0, SLAB // 256, rotate, (cosines, sines))

    def cosine_column(cb, carry):
        table_column(cb, "cos")
        return carry

    def sine_column(cb, carry):
        table_column(cb, "sin")
        return carry

    lax.fori_loop(0, 6, cosine_column, 0)
    table_column(6, "both")
    lax.fori_loop(7, 13, sine_column, 0)

    known = ids_all.at[pl.ds(0, 13)]
    pltpu.make_async_copy(known, known, id_recv_sem).wait()
    ids_all[RING + 2 * my_z + 1 - my_c] = ids_all[2 * my_y + 1 - my_c]

    def choose(m, carry):
        station = lax.broadcasted_iota(jnp.int32, (STATIONS, 128), 0)
        for line in range(2):
            for side in range(2):
                wanted = ids_all[line * RING + m, side : side + 1, :]
                hot = jnp.transpose(jnp.where(station == wanted, F32(1), F32(0))).astype(BF16)
                for i in range(SHARE // 16):
                    at, pair = i * 32 + side * 16, line * SHARE + i * 16
                    sel[line * RING + m, at : at + 16, :] = hot[pair : pair + 16]
        return carry

    lax.fori_loop(0, RING, choose, 0)

    for q in range(PARTS):
        width = WIDTHS[q]
        arrived = wr[q].at[pl.ds(0, MEMBERS - 1)]
        pltpu.make_async_copy(arrived, arrived, w_recv_sem.at[q]).wait()

        def repack(i, carry):
            both = wr[q][pl.ds(2 * i, 2)].astype(F32)
            rows = pl.ds(pl.multiple_of(i * 16, 16), 16)
            low = both[:, :8].reshape(16, width).astype(BF16)
            high = both[:, 8:].reshape(16, width).astype(BF16)
            for j in range(width // 128):
                wc[j, rows, :128] = low[:, j * 128 : (j + 1) * 128]
                wc[j, rows, 128:] = high[:, j * 128 : (j + 1) * 128]
            return carry

        lax.fori_loop(0, MEMBERS // 2, repack, 0)

        def correlate(j, carry):
            real_at = pl.ds(pl.multiple_of(j * 128, 128), 128)
            imag_at = pl.ds(pl.multiple_of(768 + j * 128, 128), 128)
            for m in range(0, BLOCKS, 8):
                both = jnp.dot(
                    sel[m : m + 8].reshape(8 * 2 * SHARE, STATIONS), wc[j], preferred_element_type=F32
                )
                for i in range(8 * SHARE // 16):
                    a0, a1 = both[i * 32 : i * 32 + 16, :128], both[i * 32 : i * 32 + 16, 128:]
                    b0, b1 = both[i * 32 + 16 : i * 32 + 32, :128], both[i * 32 + 16 : i * 32 + 32, 128:]
                    rows = slice(m * SHARE + i * 16, m * SHARE + i * 16 + 16)
                    cross[rows, real_at] = (a0 * b0 + a1 * b1).astype(BF16)
                    cross[rows, imag_at] = (a1 * b0 - a0 * b1).astype(BF16)
            return carry

        lax.fori_loop(0, width // 128, correlate, 0)

        bins = slice(STARTS[q], STARTS[q] + width)

        def add(columns, value):
            if q == 0:
                acc[:, columns] = value
            else:
                acc[:, columns] += value

        def transform(t, carry):
            left = pl.ds(pl.multiple_of(t * 256, 256), 256)
            right = pl.ds(pl.multiple_of(t * 256 + 128, 128), 256)
            far = pl.ds(pl.multiple_of(t * 256 + 896, 128), 256)
            add(left, jnp.dot(cross[:, :width], tcos[bins, left], preferred_element_type=F32))
            add(far, jnp.dot(cross[:, 768 : 768 + width], tsin[bins, right], preferred_element_type=F32))
            return carry

        lax.fori_loop(0, 3, transform, 0)
        add(
            slice(768, 896),
            jnp.dot(cross[:, :width], tcos[bins, 768:], preferred_element_type=F32)
            + jnp.dot(cross[:, 768 : 768 + width], tsin[bins, :128], preferred_element_type=F32),
        )

    places = (my_y, my_z)

    def block(line, k, c):
        return pl.ds(pl.multiple_of((line * RING + 2 * k + c) * SHARE, 16), SHARE)

    steps = [(i, line) for i in (2, 1, 3, 0) for line in range(2)]
    a_copies = [[], []]
    for p, (first, width) in enumerate(PIECES):
        for n, (i, line) in enumerate(steps):
            k = lax.rem(places[line] + i, 4)
            a_send[p][n] = acc[block(line, k, 1 - my_c), first : first + width].astype(BF16)
            copy = pltpu.make_async_remote_copy(
                src_ref=a_send[p].at[n], dst_ref=a_recv[p].at[n],
                send_sem=a_send_sem.at[p, n], recv_sem=a_recv_sem.at[p, n],
                device_id={"sta": me + 1 - 2 * my_c}, device_id_type=MESH,
            )
            copy.start()
            a_copies[p].append(copy)

    b_copies = [[], []]
    for p, (first, width) in enumerate(PIECES):
        for n, (i, line) in enumerate(steps[:6]):
            k = lax.rem(places[line] + i, 4)
            a_copies[p][n].wait_recv()
            mine = acc[block(line, k, my_c), first : first + width]
            b_send[p][n] = (mine + a_recv[p][n].astype(F32)).astype(BF16)
            peer = row + 2 * k + my_c if line == 0 else k * RING + inside
            copy = pltpu.make_async_remote_copy(
                src_ref=b_send[p].at[n], dst_ref=b_recv[p].at[n],
                send_sem=b_send_sem.at[p, n], recv_sem=b_recv_sem.at[p, n],
                device_id={"sta": peer}, device_id_type=MESH,
            )
            copy.start()
            b_copies[p].append(copy)

    meta = meta_ref[...]
    square = (128, 128)
    sub, lane = lax.broadcasted_iota(jnp.int32, square, 0), lax.broadcasted_iota(jnp.int32, square, 1)
    dest = meta[3:4, :]
    dest_across = jnp.transpose(jnp.broadcast_to(dest.astype(F32), square)).astype(jnp.int32)
    earlier = (dest_across == dest) & (sub < lane) & (sub < PAIRS)
    position = jnp.sum(jnp.where(earlier, F32(1), F32(0)), axis=0, keepdims=True).astype(jnp.int32)
    counted = (lane[0:1] < PAIRS) & (meta[2:3, :] == 1)
    code = jnp.where(counted, dest * 8 + position * SEGS, -64)

    def place(t, carry):
        target = lax.broadcasted_iota(jnp.int32, (128, 128), 0) + t * 128
        rows = pl.ds(pl.multiple_of(t * 128, 128), 128)
        for k in range(SEGS):
            gsel[rows, k * 128 : (k + 1) * 128] = jnp.where(target == code + k, F32(1), F32(0)).astype(BF16)
        return carry

    lax.fori_loop(0, DEVS * 8 // 128, place, 0)
    slot_across = jnp.transpose(jnp.broadcast_to(meta[4:5, :].astype(F32), square)).astype(BF16)
    for p in range(2):
        corr[p][...] = jnp.zeros_like(corr[p])
    corr[1][3 * 128 :, :128] = slot_across
    corr[1][3 * 128 :, 128:] = slot_across

    scale = F32(BINS ** (-0.5))
    owns = []
    for p, (first, width) in enumerate(PIECES):
        for line in range(2):
            a_copies[p][6 + line].wait_recv()
            for n in range(line, 6, 2):
                b_copies[p][n].wait_recv()
            total = acc[block(line, places[line], my_c), first : first + width]
            total = total + a_recv[p][6 + line].astype(F32)
            for n in range(line, 6, 2):
                total = total + b_recv[p][n].astype(F32)
            total = (total * scale).astype(BF16)
            for k in range(-(-width // SEG)):
                wide = min(SEG, width - k * SEG)
                at = k * 128 + line * SHARE
                corr[p][at : at + SHARE, :wide] = total[:, k * SEG : k * SEG + wide]

        def pack(t, carry):
            rows = pl.ds(pl.multiple_of(t * 256, 256), 256)
            out = jnp.dot(gsel[rows, :], corr[p][...], preferred_element_type=F32)
            c_send[p][pl.ds(t * 32, 32)] = out.reshape(32, 8, SEG).astype(BF16)
            return carry

        lax.fori_loop(0, DEVS // 32, pack, 0)
        own = pltpu.make_async_copy(c_send[p].at[dev], got[p].at[dev], own_sem.at[p])
        own.start()
        owns.append(own)

        def route(i, carry):
            peer = lax.rem(dev + i * 53, DEVS)
            pltpu.make_async_remote_copy(
                src_ref=c_send[p].at[peer], dst_ref=got[p].at[dev],
                send_sem=c_send_sem.at[p], recv_sem=c_recv_sem.at[p],
                device_id={"grp": peer // MEMBERS, "sta": lax.rem(peer, MEMBERS)},
                device_id_type=MESH,
            ).start()
            return carry

        lax.fori_loop(1, DEVS, route, 0)

    for p in range(2):
        for copy in a_copies[p]:
            copy.wait_send()
        for copy in b_copies[p]:
            copy.wait_send()
    pltpu.make_async_copy(known, known, id_send_sem).wait()
    for q in range(PARTS):
        sent = wr[q].at[pl.ds(0, MEMBERS - 1)]
        pltpu.make_async_copy(sent, sent, w_send_sem.at[q]).wait()
    for p in range(2):
        owns[p].wait()
        rest = c_send[p].at[pl.ds(0, DEVS - 1)]
        pltpu.make_async_copy(rest, rest, c_send_sem.at[p]).wait()
        pltpu.make_async_copy(rest, rest, c_recv_sem.at[p]).wait()


def correlate_and_route(x, meta):
    vmem = pl.BlockSpec(memory_space=pltpu.VMEM)
    dma = pltpu.SemaphoreType.DMA
    return pl.pallas_call(
        main_kernel,
        out_shape=[jax.ShapeDtypeStruct((DEVS, 8, SEG), BF16)] * 2,
        in_specs=[vmem] * 2,
        out_specs=[pl.BlockSpec(memory_space=pl.ANY)] * 2,
        scratch_shapes=[
            *[pltpu.VMEM((RING, 16, w), BF16) for w in WIDTHS],
            *[pltpu.VMEM((MEMBERS, 16, w), BF16) for w in WIDTHS],
            pltpu.VMEM((max(WIDTHS) // 128, STATIONS, 256), BF16),
            pltpu.VMEM((BLOCKS, 8, 128), jnp.int32),
            pltpu.VMEM((BLOCKS, 2 * SHARE, STATIONS), BF16),
            pltpu.VMEM((SLAB, 896), BF16),
            pltpu.VMEM((SLAB, 896), BF16),
            pltpu.VMEM((RING * PAIRS, COLS), F32),
            pltpu.VMEM((RING * PAIRS, 2 * max(WIDTHS)), BF16),
            *[pltpu.VMEM((8, SHARE, w), BF16) for _ in range(2) for _, w in PIECES],
            *[pltpu.VMEM((6, SHARE, w), BF16) for _ in range(2) for _, w in PIECES],
            *[pltpu.VMEM((SEGS * 128, SEG), BF16) for _ in range(2)],
            pltpu.VMEM((DEVS * 8, SEGS * 128), BF16),
            *[pltpu.VMEM((DEVS, 8, SEG), BF16) for _ in range(2)],
            dma, dma,
            dma((PARTS,)), dma((PARTS,)),
            dma((2, 8)), dma((2, 8)),
            dma((2, 6)), dma((2, 6)),
            dma((2,)), dma((2,)), dma((2,)),
        ],
        compiler_params=pltpu.CompilerParams(
            collective_id=0, has_side_effects=True, vmem_limit_bytes=46 * 1024 * 1024
        ),
    )(x, meta)


def stack_kernel(got_a, got_b, stacks_ref, out_ref):
    rows = DEVS * 8
    got = [ref[...].reshape(rows, SEG) for ref in (got_a, got_b)]
    first = jnp.where(lax.broadcasted_iota(jnp.int32, (8, SEG), 1) == 0, F32(1), F32(0)).astype(BF16)
    marks = lax.dot_general(first, got[1], (((1,), (1,)), ((), ())), preferred_element_type=F32)
    place = lax.broadcasted_iota(jnp.int32, (8, rows), 1) & 3
    marks = jnp.where(place == 3, marks, F32(0))
    marks = jnp.maximum(marks, pltpu.roll(marks, rows - 1, 1))
    marks = jnp.maximum(marks, pltpu.roll(marks, rows - 2, 1))
    code = (marks.astype(jnp.int32) + place * PAIRS)[0:1]
    parts = [[], []]
    for k in range(SEGS):
        want = lax.broadcasted_iota(jnp.int32, (PAIRS, rows), 0) + k * PAIRS
        hot = jnp.where(want == code, F32(1), F32(0)).astype(BF16)
        for p in range(2 if k < 3 else 1):
            parts[p].append(jnp.dot(hot, got[p], preferred_element_type=F32))
    parts = parts[0] + parts[1]
    sums = jnp.concatenate(parts, axis=1)
    even, odd = sums[:, :896], sums[:, SIDE : SIDE + 896]
    tiles = 7
    gap = even - odd
    high = gap.astype(BF16)
    low = (gap - high.astype(F32)).astype(BF16)
    stack = jnp.concatenate(
        [v[:, t * 128 : (t + 1) * 128] for v in (high, low) for t in range(tiles)], axis=0
    )
    mirror = lax.broadcasted_iota(jnp.int32, (128, 128), 0) + lax.broadcasted_iota(jnp.int32, (128, 128), 1)
    mirror = jnp.where(mirror == 127, F32(1), F32(0)).astype(BF16)
    turned = jnp.dot(stack, mirror, preferred_element_type=F32)
    turned = turned[: tiles * PAIRS] + turned[tiles * PAIRS :]
    behind = jnp.concatenate(
        [turned[t * PAIRS : (t + 1) * PAIRS] for t in reversed(range(tiles))], axis=1
    )
    skip = tiles * 128 - HALF
    out_ref[:, :HALF] = stacks_ref[:, :HALF] + behind[:, skip:]
    out_ref[:, HALF:] = stacks_ref[:, HALF:] + (even + odd)[:, 1:HALF]


def add_rows(got_a, got_b, stacks):
    vmem = pl.BlockSpec(memory_space=pltpu.VMEM)
    return pl.pallas_call(
        stack_kernel,
        out_shape=jax.ShapeDtypeStruct(stacks.shape, F32),
        in_specs=[vmem] * 3,
        out_specs=vmem,
        compiler_params=pltpu.CompilerParams(vmem_limit_bytes=40 * 1024 * 1024),
    )(got_a, got_b, stacks)


def local(spectra, stacks, pair_sta, pair_valid, owner, slot):
    rows = [pair_sta, pair_valid[None, :], owner.reshape(1, PAIRS), slot[None, :]]
    meta = jnp.pad(jnp.concatenate(rows, axis=0), ((0, 3), (0, 128 - PAIRS)))
    got_a, got_b = correlate_and_route(spectra, meta)
    return add_rows(got_a, got_b, stacks)


def solution(mesh):
    return jax.shard_map(
        local,
        mesh=mesh,
        in_specs=(
            P(("grp", "sta"), None, None),
            P(("grp", "sta"), None),
            P(None, ("grp", "sta")),
            P(("grp", "sta")),
            P(("grp", "sta"), None),
            P(("grp", "sta")),
        ),
        out_specs=P(("grp", "sta"), None),
        check_vma=False,
    )
```

```python
import functools
import math

import jax
import jax.numpy as jnp
from jax import lax
from jax.experimental import pallas as pl
from jax.experimental.pallas import tpu as pltpu
from jax.sharding import PartitionSpec as P

BAND = 64
MESH = pl.DeviceIdType.MESH
BF16 = jnp.bfloat16
F32 = jnp.float32

BINS = 18432
LAGS = 1601
HALF = (LAGS + 1) // 2
SIDE = 832
COLS = 2 * SIDE
PAIRS = 96
SHARE = PAIRS // 2
RING = 8
BLOCKS = 2 * RING
SLAB = BINS // RING
WIDTHS = (512, 512, 512, 512, 256)
STARTS = (0, 512, 1024, 1536, 2048)
WIDE = max(WIDTHS)
PARTS = len(WIDTHS)
MEMBERS = 32
GROUPS = 4
DEVS = 128
STATIONS = 256
SEG = 256
SEGS = 4
PIECES = ((1024, 640), (0, 1024))


def angles(freqs, shifts):
    product = (freqs * shifts).astype(F32)
    turns = jnp.floor(product * F32(1.0 / (2 * BINS)))
    return (product - turns * F32(2 * BINS)) * F32(math.pi / BINS)


def main_kernel(spectra_ref, pair_ref, valid_ref, owner_ref, slot_ref, got_a, got_b, *scratch):
    ws, wr = scratch[:PARTS], scratch[PARTS : 2 * PARTS]
    (
        x_ref, meta_ref, wc, ids_all, sel, tcos, tsin, acc, cross,
        a_send_0, a_send_1, a_recv_0, a_recv_1, b_send_0, b_send_1, b_recv_0, b_recv_1,
        corr_0, corr_1, gsel, c_send_0, c_send_1,
        id_send_sem, id_recv_sem, w_send_sem, w_recv_sem,
        a_send_sem, a_recv_sem, b_send_sem, b_recv_sem, c_send_sem, c_recv_sem, own_sem, x_sem,
    ) = scratch[2 * PARTS :]
    a_send, a_recv = (a_send_0, a_send_1), (a_recv_0, a_recv_1)
    b_send, b_recv = (b_send_0, b_send_1), (b_recv_0, b_recv_1)
    corr, c_send, got = (corr_0, corr_1), (c_send_0, c_send_1), (got_a, got_b)
    grp = lax.axis_index("grp")
    me = lax.axis_index("sta")
    dev = grp * MEMBERS + me
    my_z, inside = me // RING, lax.rem(me, RING)
    my_y, my_c = inside // 2, lax.rem(inside, 2)

    def slab_of(member):
        z, rest = member // RING, lax.rem(member, RING)
        return 2 * lax.rem(z + rest // 2, 4) + lax.rem(rest, 2)

    my_slab = slab_of(me)
    row = me - inside

    def load(s):
        bins = pl.ds(pl.multiple_of(s * SLAB, 128), SLAB)
        return pltpu.make_async_copy(spectra_ref.at[:, :, bins], x_ref.at[:, :, bins], x_sem.at[s])

    for s in range(RING):
        load(s).start()

    barrier = pltpu.get_barrier_semaphore()

    def greet(i, carry):
        peer = lax.rem(dev + i, DEVS)
        pl.semaphore_signal(
            barrier, inc=1,
            device_id={"grp": peer // MEMBERS, "sta": lax.rem(peer, MEMBERS)},
            device_id_type=MESH,
        )
        return carry

    lax.fori_loop(1, DEVS, greet, 0)

    meta_ref[...] = jnp.zeros_like(meta_ref)
    meta_ref[0:2, :PAIRS] = pair_ref[...]
    meta_ref[2:3, :PAIRS] = valid_ref[...]
    meta_ref[3:4, :PAIRS] = owner_ref[...]
    meta_ref[4:5, :PAIRS] = slot_ref[...]

    lane = lax.broadcasted_iota(jnp.int32, (128, 128), 1) // BAND
    sub = lax.broadcasted_iota(jnp.int32, (128, 128), 0) // BAND
    bands = jnp.where(lane == sub, F32(1), F32(0))

    def whiten(s, carry):
        load(s).wait()
        base = pl.multiple_of(s * SLAB, 128)
        x0 = x_ref[:, 0, pl.ds(base, SLAB)]
        x1 = x_ref[:, 1, pl.ds(base, SLAB)]
        square = x0 * x0 + x1 * x1
        tiles = SLAB // 128
        rows = jnp.concatenate([square[:, j * 128 : (j + 1) * 128] for j in range(tiles)], axis=0)
        power = jnp.dot(
            rows, bands, precision=lax.Precision.HIGHEST, preferred_element_type=F32
        ) * F32(1.0 / (2 * BAND))
        inverse = lax.rsqrt(power + F32(1e-06))
        for j in range(tiles):
            inv = inverse[j * 8 : (j + 1) * 8]
            cut = slice(j * 128, (j + 1) * 128)
            both = jnp.concatenate([x0[:, cut] * inv, x1[:, cut] * inv], axis=0).astype(BF16)
            q = max(p for p in range(PARTS) if STARTS[p] <= j * 128)
            o = j * 128 - STARTS[q]
            ws[q][s, :, o : o + 128] = both
        return carry

    lax.fori_loop(0, RING, whiten, 0)
    pl.semaphore_wait(barrier, DEVS - 1)

    def send_ids(slot, peer):
        pltpu.make_async_remote_copy(
            src_ref=meta_ref, dst_ref=ids_all.at[slot],
            send_sem=id_send_sem, recv_sem=id_recv_sem,
            device_id={"sta": peer}, device_id_type=MESH,
        ).start()

    def along_y(i, carry):
        send_ids(inside, row + lax.rem(inside + i, RING))
        return carry

    def along_z(i, carry):
        send_ids(RING + 2 * my_z + my_c, lax.rem(my_z + 1 + i // 2, 4) * RING + 2 * my_y + lax.rem(i, 2))
        return carry

    lax.fori_loop(1, RING, along_y, 0)
    lax.fori_loop(0, 6, along_z, 0)
    ids_all[inside] = meta_ref[...]
    ids_all[RING + 2 * my_z + my_c] = meta_ref[...]

    def send_part(q):
        def one(i, carry):
            peer = lax.rem(me + i * 11, MEMBERS)
            pltpu.make_async_remote_copy(
                src_ref=ws[q].at[slab_of(peer)], dst_ref=wr[q].at[me],
                send_sem=w_send_sem.at[q], recv_sem=w_recv_sem.at[q],
                device_id={"sta": peer}, device_id_type=MESH,
            ).start()
            return carry

        lax.fori_loop(1, MEMBERS, one, 0)
        wr[q][me] = ws[q][my_slab]

    for q in range(PARTS):
        send_part(q)

    start = my_slab * SLAB

    def table_column(cb, half):
        column = lax.broadcasted_iota(jnp.int32, (64, 128), 1) + cb * 128
        cosine_side = column < SIDE
        lags = jnp.where(cosine_side, column, column - SIDE)
        freqs = lax.broadcasted_iota(jnp.int32, (64, 128), 0) + start
        theta = angles(freqs, lags)
        cosines, sines = jnp.cos(theta), jnp.sin(theta)
        turn = angles(jnp.full((8, 128), 64, jnp.int32), lags[:8])
        tc = jnp.concatenate([jnp.cos(turn)] * 8, axis=0)
        ts = jnp.concatenate([jnp.sin(turn)] * 8, axis=0)

        def rotate(i, state):
            c, s = state
            for step in range(4):
                rows = pl.ds(pl.multiple_of(i * 256 + step * 64, 64), 64)
                if half == "both":
                    tcos[rows, SIDE - 64 : SIDE + 64] = jnp.where(cosine_side, c, F32(0)).astype(BF16)
                    tsin[rows, :128] = jnp.where(cosine_side, F32(0), -s).astype(BF16)
                elif half == "cos":
                    tcos[rows, pl.ds(pl.multiple_of(cb * 128, 128), 128)] = c.astype(BF16)
                else:
                    tsin[rows, pl.ds(pl.multiple_of(cb * 128 - 768, 128), 128)] = (-s).astype(BF16)
                c, s = c * tc - s * ts, s * tc + c * ts
            return c, s

        lax.fori_loop(0, SLAB // 256, rotate, (cosines, sines))

    def cosine_column(cb, carry):
        table_column(cb, "cos")
        return carry

    def sine_column(cb, carry):
        table_column(cb, "sin")
        return carry

    lax.fori_loop(0, 6, cosine_column, 0)
    table_column(6, "both")
    lax.fori_loop(7, 13, sine_column, 0)

    known = ids_all.at[pl.ds(0, 13)]
    pltpu.make_async_copy(known, known, id_recv_sem).wait()
    ids_all[RING + 2 * my_z + 1 - my_c] = ids_all[2 * my_y + 1 - my_c]

    def choose(m, carry):
        station = lax.broadcasted_iota(jnp.int32, (STATIONS, 128), 0)
        for line in range(2):
            for side in range(2):
                wanted = ids_all[line * RING + m, side : side + 1, :]
                hot = jnp.transpose(jnp.where(station == wanted, F32(1), F32(0))).astype(BF16)
                for i in range(SHARE // 16):
                    at, pair = i * 32 + side * 16, line * SHARE + i * 16
                    sel[line * RING + m, at : at + 16, :] = hot[pair : pair + 16]
        return carry

    lax.fori_loop(0, RING, choose, 0)

    meta = meta_ref[...]
    square = (128, 128)
    sub, lane = lax.broadcasted_iota(jnp.int32, square, 0), lax.broadcasted_iota(jnp.int32, square, 1)
    dest = meta[3:4, :]
    dest_across = jnp.transpose(jnp.broadcast_to(dest.astype(F32), square)).astype(jnp.int32)
    earlier = (dest_across == dest) & (sub < lane) & (sub < PAIRS)
    position = jnp.sum(jnp.where(earlier, F32(1), F32(0)), axis=0, keepdims=True).astype(jnp.int32)
    counted = (lane[0:1] < PAIRS) & (meta[2:3, :] == 1)
    code = jnp.where(counted, dest * 8 + position * SEGS, -64)

    def place(t, carry):
        target = lax.broadcasted_iota(jnp.int32, (128, 128), 0) + t * 128
        rows = pl.ds(pl.multiple_of(t * 128, 128), 128)
        for k in range(SEGS):
            gsel[rows, k * 128 : (k + 1) * 128] = jnp.where(target == code + k, F32(1), F32(0)).astype(BF16)
        return carry

    lax.fori_loop(0, DEVS * 8 // 128, place, 0)
    slot_across = jnp.transpose(jnp.broadcast_to(meta[4:5, :].astype(F32), square)).astype(BF16)
    for p in range(2):
        corr[p][...] = jnp.zeros_like(corr[p])
    corr[0][3 * 128 :, :128] = slot_across
    corr[0][3 * 128 :, 128:] = slot_across

    places = (my_y, my_z)

    def block(line, k, c):
        return pl.ds(pl.multiple_of((line * RING + 2 * k + c) * SHARE, 16), SHARE)

    steps = [(i, line) for i in (2, 1, 3, 0) for line in range(2)]
    a_copies = [[], []]

    def send_a(p):
        first, width = PIECES[p]
        for n, (i, line) in enumerate(steps):
            k = lax.rem(places[line] + i, 4)
            a_send[p][n] = acc[block(line, k, 1 - my_c), first : first + width].astype(BF16)
            copy = pltpu.make_async_remote_copy(
                src_ref=a_send[p].at[n], dst_ref=a_recv[p].at[n],
                send_sem=a_send_sem.at[p, n], recv_sem=a_recv_sem.at[p, n],
                device_id={"sta": me + 1 - 2 * my_c}, device_id_type=MESH,
            )
            copy.start()
            a_copies[p].append(copy)

    for q in range(PARTS):
        width = WIDTHS[q]
        arrived = wr[q].at[pl.ds(0, MEMBERS - 1)]
        pltpu.make_async_copy(arrived, arrived, w_recv_sem.at[q]).wait()

        def repack(i, carry):
            both = wr[q][pl.ds(2 * i, 2)].astype(F32)
            rows = pl.ds(pl.multiple_of(i * 16, 16), 16)
            low = both[:, :8].reshape(16, width).astype(BF16)
            high = both[:, 8:].reshape(16, width).astype(BF16)
            for j in range(width // 128):
                wc[j, rows, :128] = low[:, j * 128 : (j + 1) * 128]
                wc[j, rows, 128:] = high[:, j * 128 : (j + 1) * 128]
            return carry

        lax.fori_loop(0, MEMBERS // 2, repack, 0)

        def correlate(pair, carry):
            for j in (2 * pair, 2 * pair + 1):
                real_at = pl.ds(pl.multiple_of(j * 128, 128), 128)
                imag_at = pl.ds(pl.multiple_of(WIDE + j * 128, 128), 128)
                for m in range(0, BLOCKS, 8):
                    both = jnp.dot(
                        sel[m : m + 8].reshape(8 * 2 * SHARE, STATIONS), wc[j], preferred_element_type=F32
                    )
                    for i in range(8 * SHARE // 16):
                        a0, a1 = both[i * 32 : i * 32 + 16, :128], both[i * 32 : i * 32 + 16, 128:]
                        b0, b1 = both[i * 32 + 16 : i * 32 + 32, :128], both[i * 32 + 16 : i * 32 + 32, 128:]
                        rows = slice(m * SHARE + i * 16, m * SHARE + i * 16 + 16)
                        cross[rows, real_at] = (a0 * b0 + a1 * b1).astype(BF16)
                        cross[rows, imag_at] = (a1 * b0 - a0 * b1).astype(BF16)
            return carry

        lax.fori_loop(0, width // 256, correlate, 0)

        bins = slice(STARTS[q], STARTS[q] + width)

        def add(columns, value):
            if q == 0:
                acc[:, columns] = value
            else:
                acc[:, columns] += value

        real, imag = cross.at[:, :width], cross.at[:, WIDE : WIDE + width]
        add(slice(896, COLS), jnp.dot(imag[...], tsin[bins, 128:], preferred_element_type=F32))
        if q == PARTS - 1:
            send_a(0)
        add(slice(0, 768), jnp.dot(real[...], tcos[bins, :768], preferred_element_type=F32))
        add(
            slice(768, 896),
            jnp.dot(real[...], tcos[bins, 768:], preferred_element_type=F32)
            + jnp.dot(imag[...], tsin[bins, :128], preferred_element_type=F32),
        )
        if q == PARTS - 1:
            send_a(1)

    b_copies = [[], []]
    for p, (first, width) in enumerate(PIECES):
        for n, (i, line) in enumerate(steps[:6]):
            k = lax.rem(places[line] + i, 4)
            a_copies[p][n].wait_recv()
            mine = acc[block(line, k, my_c), first : first + width]
            b_send[p][n] = (mine + a_recv[p][n].astype(F32)).astype(BF16)
            peer = row + 2 * k + my_c if line == 0 else k * RING + inside
            copy = pltpu.make_async_remote_copy(
                src_ref=b_send[p].at[n], dst_ref=b_recv[p].at[n],
                send_sem=b_send_sem.at[p, n], recv_sem=b_recv_sem.at[p, n],
                device_id={"sta": peer}, device_id_type=MESH,
            )
            copy.start()
            b_copies[p].append(copy)

    scale = F32(BINS ** (-0.5))
    owns = []
    for p, (first, width) in enumerate(PIECES):
        for line in range(2):
            a_copies[p][6 + line].wait_recv()
            for n in range(line, 6, 2):
                b_copies[p][n].wait_recv()
            total = acc[block(line, places[line], my_c), first : first + width]
            total = total + a_recv[p][6 + line].astype(F32)
            for n in range(line, 6, 2):
                total = total + b_recv[p][n].astype(F32)
            total = (total * scale).astype(BF16)
            for k in range(-(-width // SEG)):
                wide = min(SEG, width - k * SEG)
                at = k * 128 + line * SHARE
                corr[p][at : at + SHARE, :wide] = total[:, k * SEG : k * SEG + wide]

        def pack(t, carry):
            rows = pl.ds(pl.multiple_of(t * 256, 256), 256)
            out = jnp.dot(gsel[rows, :], corr[p][...], preferred_element_type=F32)
            c_send[p][pl.ds(t * 32, 32)] = out.reshape(32, 8, SEG).astype(BF16)
            return carry

        lax.fori_loop(0, DEVS // 32, pack, 0)
        own = pltpu.make_async_copy(c_send[p].at[dev], got[p].at[dev], own_sem.at[p])
        own.start()
        owns.append(own)

        def route(i, carry):
            peer = lax.rem(dev + i * 53, DEVS)
            pltpu.make_async_remote_copy(
                src_ref=c_send[p].at[peer], dst_ref=got[p].at[dev],
                send_sem=c_send_sem.at[p], recv_sem=c_recv_sem.at[p],
                device_id={"grp": peer // MEMBERS, "sta": lax.rem(peer, MEMBERS)},
                device_id_type=MESH,
            ).start()
            return carry

        lax.fori_loop(1, DEVS, route, 0)

    for p in range(2):
        for copy in a_copies[p]:
            copy.wait_send()
        for copy in b_copies[p]:
            copy.wait_send()
    pltpu.make_async_copy(known, known, id_send_sem).wait()
    for q in range(PARTS):
        sent = wr[q].at[pl.ds(0, MEMBERS - 1)]
        pltpu.make_async_copy(sent, sent, w_send_sem.at[q]).wait()
    for p in range(2):
        owns[p].wait()
        rest = c_send[p].at[pl.ds(0, DEVS - 1)]
        pltpu.make_async_copy(rest, rest, c_send_sem.at[p]).wait()
        pltpu.make_async_copy(rest, rest, c_recv_sem.at[p]).wait()


def correlate_and_route(*operands):
    vmem = pl.BlockSpec(memory_space=pltpu.VMEM)
    dma = pltpu.SemaphoreType.DMA
    return pl.pallas_call(
        main_kernel,
        out_shape=[jax.ShapeDtypeStruct((DEVS, 8, SEG), BF16)] * 2,
        in_specs=[pl.BlockSpec(memory_space=pltpu.HBM)] + [vmem] * 4,
        out_specs=[pl.BlockSpec(memory_space=pl.ANY)] * 2,
        scratch_shapes=[
            *[pltpu.VMEM((RING, 16, w), BF16) for w in WIDTHS],
            *[pltpu.VMEM((MEMBERS, 16, w), BF16) for w in WIDTHS],
            pltpu.VMEM((RING, 2, BINS), F32),
            pltpu.VMEM((8, 128), jnp.int32),
            pltpu.VMEM((WIDE // 128, STATIONS, 256), BF16),
            pltpu.VMEM((BLOCKS, 8, 128), jnp.int32),
            pltpu.VMEM((BLOCKS, 2 * SHARE, STATIONS), BF16),
            pltpu.VMEM((SLAB, 896), BF16),
            pltpu.VMEM((SLAB, 896), BF16),
            pltpu.VMEM((RING * PAIRS, COLS), F32),
            pltpu.VMEM((RING * PAIRS, 2 * WIDE), BF16),
            *[pltpu.VMEM((8, SHARE, w), BF16) for _ in range(2) for _, w in PIECES],
            *[pltpu.VMEM((6, SHARE, w), BF16) for _ in range(2) for _, w in PIECES],
            *[pltpu.VMEM((SEGS * 128, SEG), BF16) for _ in range(2)],
            pltpu.VMEM((DEVS * 8, SEGS * 128), BF16),
            *[pltpu.VMEM((DEVS, 8, SEG), BF16) for _ in range(2)],
            dma, dma,
            dma((PARTS,)), dma((PARTS,)),
            dma((2, 8)), dma((2, 8)),
            dma((2, 6)), dma((2, 6)),
            dma((2,)), dma((2,)), dma((2,)), dma((RING,)),
        ],
        compiler_params=pltpu.CompilerParams(
            collective_id=0, has_side_effects=True, vmem_limit_bytes=46 * 1024 * 1024
        ),
    )(*operands)


def stack_kernel(got_a, got_b, stacks_ref, out_ref):
    rows = DEVS * 8
    got = [ref[...].reshape(rows, SEG) for ref in (got_a, got_b)]
    first = jnp.where(lax.broadcasted_iota(jnp.int32, (8, SEG), 1) == 0, F32(1), F32(0)).astype(BF16)
    marks = lax.dot_general(first, got[0], (((1,), (1,)), ((), ())), preferred_element_type=F32)
    place = lax.broadcasted_iota(jnp.int32, (8, rows), 1) & 3
    marks = jnp.where(place == 3, marks, F32(0))
    marks = jnp.maximum(marks, pltpu.roll(marks, rows - 1, 1))
    marks = jnp.maximum(marks, pltpu.roll(marks, rows - 2, 1))
    code = (marks.astype(jnp.int32) + place * PAIRS)[0:1]
    parts = [[], []]
    for k in range(SEGS):
        want = lax.broadcasted_iota(jnp.int32, (PAIRS, rows), 0) + k * PAIRS
        hot = jnp.where(want == code, F32(1), F32(0)).astype(BF16)
        for p in range(0 if k < 3 else 1, 2):
            parts[p].append(jnp.dot(hot, got[p], preferred_element_type=F32))
    parts = parts[1] + parts[0]
    sums = jnp.concatenate(parts, axis=1)
    even, odd = sums[:, :896], sums[:, SIDE : SIDE + 896]
    tiles = 7
    gap = even - odd
    high = gap.astype(BF16)
    low = (gap - high.astype(F32)).astype(BF16)
    stack = jnp.concatenate(
        [v[:, t * 128 : (t + 1) * 128] for v in (high, low) for t in range(tiles)], axis=0
    )
    mirror = lax.broadcasted_iota(jnp.int32, (128, 128), 0) + lax.broadcasted_iota(jnp.int32, (128, 128), 1)
    mirror = jnp.where(mirror == 127, F32(1), F32(0)).astype(BF16)
    turned = jnp.dot(stack, mirror, preferred_element_type=F32)
    turned = turned[: tiles * PAIRS] + turned[tiles * PAIRS :]
    behind = jnp.concatenate(
        [turned[t * PAIRS : (t + 1) * PAIRS] for t in reversed(range(tiles))], axis=1
    )
    skip = tiles * 128 - HALF
    out_ref[:, :HALF] = stacks_ref[:, :HALF] + behind[:, skip:]
    out_ref[:, HALF:] = stacks_ref[:, HALF:] + (even + odd)[:, 1:HALF]


def add_rows(got_a, got_b, stacks):
    vmem = pl.BlockSpec(memory_space=pltpu.VMEM)
    return pl.pallas_call(
        stack_kernel,
        out_shape=jax.ShapeDtypeStruct(stacks.shape, F32),
        in_specs=[vmem] * 3,
        out_specs=vmem,
        compiler_params=pltpu.CompilerParams(vmem_limit_bytes=40 * 1024 * 1024),
    )(got_a, got_b, stacks)


def local(spectra, stacks, pair_sta, pair_valid, owner, slot):
    got_a, got_b = correlate_and_route(
        spectra, pair_sta, pair_valid[None, :], owner.reshape(1, PAIRS), slot[None, :]
    )
    return add_rows(got_a, got_b, stacks)


def solution(mesh):
    return jax.shard_map(
        local,
        mesh=mesh,
        in_specs=(
            P(("grp", "sta"), None, None),
            P(("grp", "sta"), None),
            P(None, ("grp", "sta")),
            P(("grp", "sta")),
            P(("grp", "sta"), None),
            P(("grp", "sta")),
        ),
        out_specs=P(("grp", "sta"), None),
        check_vma=False,
    )
```

```python
import functools
import math

import jax
import jax.numpy as jnp
from jax import lax
from jax.experimental import pallas as pl
from jax.experimental.pallas import tpu as pltpu
from jax.sharding import PartitionSpec as P

BAND = 64
MESH = pl.DeviceIdType.MESH
BF16 = jnp.bfloat16
F32 = jnp.float32

BINS = 18432
LAGS = 1601
HALF = (LAGS + 1) // 2
SIDE = 832
COLS = 2 * SIDE
PAIRS = 96
SHARE = PAIRS // 2
RING = 8
BLOCKS = 2 * RING
SLAB = BINS // RING
WIDTHS = (512, 512, 512, 512, 256)
STARTS = (0, 512, 1024, 1536, 2048)
WIDE = max(WIDTHS)
PARTS = len(WIDTHS)
MEMBERS = 32
GROUPS = 4
DEVS = 128
STATIONS = 256
SEG = 256
SEGS = 4
PIECES = ((1024, 640), (0, 1024))


def angles(freqs, shifts):
    product = (freqs * shifts).astype(F32)
    turns = jnp.floor(product * F32(1.0 / (2 * BINS)))
    return (product - turns * F32(2 * BINS)) * F32(math.pi / BINS)


def main_kernel(spectra_ref, meta_ref, got_a, got_b, *scratch):
    ws, wr = scratch[:PARTS], scratch[PARTS : 2 * PARTS]
    (
        x_ref, wc, ids_all, sel, tcos, tsin, acc, cross,
        a_send_0, a_send_1, a_recv_0, a_recv_1, b_send_0, b_send_1, b_recv_0, b_recv_1,
        corr_0, corr_1, gsel, c_send_0, c_send_1,
        id_send_sem, id_recv_sem, w_send_sem, w_recv_sem,
        a_send_sem, a_recv_sem, b_send_sem, b_recv_sem, c_send_sem, c_recv_sem, own_sem, x_sem,
    ) = scratch[2 * PARTS :]
    a_send, a_recv = (a_send_0, a_send_1), (a_recv_0, a_recv_1)
    b_send, b_recv = (b_send_0, b_send_1), (b_recv_0, b_recv_1)
    corr, c_send, got = (corr_0, corr_1), (c_send_0, c_send_1), (got_a, got_b)
    grp = lax.axis_index("grp")
    me = lax.axis_index("sta")
    dev = grp * MEMBERS + me
    my_z, inside = me // RING, lax.rem(me, RING)
    my_y, my_c = inside // 2, lax.rem(inside, 2)

    def slab_of(member):
        z, rest = member // RING, lax.rem(member, RING)
        return 2 * lax.rem(z + rest // 2, 4) + lax.rem(rest, 2)

    my_slab = slab_of(me)
    row = me - inside

    def load(s):
        bins = pl.ds(pl.multiple_of(s * SLAB, 128), SLAB)
        return pltpu.make_async_copy(spectra_ref.at[:, :, bins], x_ref.at[:, :, bins], x_sem.at[s])

    for s in range(RING):
        load(s).start()

    barrier = pltpu.get_barrier_semaphore()

    def greet(i, carry):
        peer = lax.rem(dev + i, DEVS)
        pl.semaphore_signal(
            barrier, inc=1,
            device_id={"grp": peer // MEMBERS, "sta": lax.rem(peer, MEMBERS)},
            device_id_type=MESH,
        )
        return carry

    lax.fori_loop(1, DEVS, greet, 0)

    lane = lax.broadcasted_iota(jnp.int32, (128, 128), 1) // BAND
    sub = lax.broadcasted_iota(jnp.int32, (128, 128), 0) // BAND
    bands = jnp.where(lane == sub, F32(1), F32(0))

    def whiten(s, carry):
        load(s).wait()
        base = pl.multiple_of(s * SLAB, 128)
        x0 = x_ref[:, 0, pl.ds(base, SLAB)]
        x1 = x_ref[:, 1, pl.ds(base, SLAB)]
        square = x0 * x0 + x1 * x1
        tiles = SLAB // 128
        rows = jnp.concatenate([square[:, j * 128 : (j + 1) * 128] for j in range(tiles)], axis=0)
        power = jnp.dot(
            rows, bands, precision=lax.Precision.HIGHEST, preferred_element_type=F32
        ) * F32(1.0 / (2 * BAND))
        inverse = lax.rsqrt(power + F32(1e-06))
        for j in range(tiles):
            inv = inverse[j * 8 : (j + 1) * 8]
            cut = slice(j * 128, (j + 1) * 128)
            both = jnp.concatenate([x0[:, cut] * inv, x1[:, cut] * inv], axis=0).astype(BF16)
            q = max(p for p in range(PARTS) if STARTS[p] <= j * 128)
            o = j * 128 - STARTS[q]
            ws[q][s, :, o : o + 128] = both
        return carry

    lax.fori_loop(0, RING, whiten, 0)
    pl.semaphore_wait(barrier, DEVS - 1)

    def send_ids(slot, peer):
        pltpu.make_async_remote_copy(
            src_ref=meta_ref, dst_ref=ids_all.at[slot],
            send_sem=id_send_sem, recv_sem=id_recv_sem,
            device_id={"sta": peer}, device_id_type=MESH,
        ).start()

    def along_y(i, carry):
        send_ids(inside, row + lax.rem(inside + i, RING))
        return carry

    def along_z(i, carry):
        send_ids(RING + 2 * my_z + my_c, lax.rem(my_z + 1 + i // 2, 4) * RING + 2 * my_y + lax.rem(i, 2))
        return carry

    lax.fori_loop(1, RING, along_y, 0)
    lax.fori_loop(0, 6, along_z, 0)
    ids_all[inside] = meta_ref[...]
    ids_all[RING + 2 * my_z + my_c] = meta_ref[...]

    def send_part(q):
        def one(i, carry):
            peer = lax.rem(me + i * 11, MEMBERS)
            pltpu.make_async_remote_copy(
                src_ref=ws[q].at[slab_of(peer)], dst_ref=wr[q].at[me],
                send_sem=w_send_sem.at[q], recv_sem=w_recv_sem.at[q],
                device_id={"sta": peer}, device_id_type=MESH,
            ).start()
            return carry

        lax.fori_loop(1, MEMBERS, one, 0)
        wr[q][me] = ws[q][my_slab]

    for q in range(PARTS):
        send_part(q)

    start = my_slab * SLAB

    def table_column(cb, half):
        column = lax.broadcasted_iota(jnp.int32, (64, 128), 1) + cb * 128
        cosine_side = column < SIDE
        lags = jnp.where(cosine_side, column, column - SIDE)
        freqs = lax.broadcasted_iota(jnp.int32, (64, 128), 0) + start
        theta = angles(freqs, lags)
        cosines, sines = jnp.cos(theta), jnp.sin(theta)
        turn = angles(jnp.full((8, 128), 64, jnp.int32), lags[:8])
        tc = jnp.concatenate([jnp.cos(turn)] * 8, axis=0)
        ts = jnp.concatenate([jnp.sin(turn)] * 8, axis=0)

        def rotate(i, state):
            c, s = state
            for step in range(4):
                rows = pl.ds(pl.multiple_of(i * 256 + step * 64, 64), 64)
                if half == "both":
                    tcos[rows, SIDE - 64 : SIDE + 64] = jnp.where(cosine_side, c, F32(0)).astype(BF16)
                    tsin[rows, :128] = jnp.where(cosine_side, F32(0), -s).astype(BF16)
                elif half == "cos":
                    tcos[rows, pl.ds(pl.multiple_of(cb * 128, 128), 128)] = c.astype(BF16)
                else:
                    tsin[rows, pl.ds(pl.multiple_of(cb * 128 - 768, 128), 128)] = (-s).astype(BF16)
                c, s = c * tc - s * ts, s * tc + c * ts
            return c, s

        lax.fori_loop(0, SLAB // 256, rotate, (cosines, sines))

    def cosine_column(cb, carry):
        table_column(cb, "cos")
        return carry

    def sine_column(cb, carry):
        table_column(cb, "sin")
        return carry

    lax.fori_loop(0, 6, cosine_column, 0)
    table_column(6, "both")
    lax.fori_loop(7, 13, sine_column, 0)

    known = ids_all.at[pl.ds(0, 13)]
    pltpu.make_async_copy(known, known, id_recv_sem).wait()
    ids_all[RING + 2 * my_z + 1 - my_c] = ids_all[2 * my_y + 1 - my_c]

    def choose(m, carry):
        station = lax.broadcasted_iota(jnp.int32, (STATIONS, 128), 0)
        for line in range(2):
            for side in range(2):
                wanted = ids_all[line * RING + m, side : side + 1, :]
                hot = jnp.transpose(jnp.where(station == wanted, F32(1), F32(0))).astype(BF16)
                for i in range(SHARE // 16):
                    at, pair = i * 32 + side * 16, line * SHARE + i * 16
                    sel[line * RING + m, at : at + 16, :] = hot[pair : pair + 16]
        return carry

    lax.fori_loop(0, RING, choose, 0)

    meta = meta_ref[...]
    square = (128, 128)
    sub, lane = lax.broadcasted_iota(jnp.int32, square, 0), lax.broadcasted_iota(jnp.int32, square, 1)
    dest = meta[3:4, :]
    dest_across = jnp.transpose(jnp.broadcast_to(dest.astype(F32), square)).astype(jnp.int32)
    earlier = (dest_across == dest) & (sub < lane) & (sub < PAIRS)
    position = jnp.sum(jnp.where(earlier, F32(1), F32(0)), axis=0, keepdims=True).astype(jnp.int32)
    counted = (lane[0:1] < PAIRS) & (meta[2:3, :] == 1)
    code = jnp.where(counted, dest * 8 + position * SEGS, -64)

    def place(t, carry):
        target = lax.broadcasted_iota(jnp.int32, (128, 128), 0) + t * 128
        rows = pl.ds(pl.multiple_of(t * 128, 128), 128)
        for k in range(SEGS):
            gsel[rows, k * 128 : (k + 1) * 128] = jnp.where(target == code + k, F32(1), F32(0)).astype(BF16)
        return carry

    lax.fori_loop(0, DEVS * 8 // 128, place, 0)
    slot_across = jnp.transpose(jnp.broadcast_to(meta[4:5, :].astype(F32), square)).astype(BF16)
    for p in range(2):
        corr[p][...] = jnp.zeros_like(corr[p])
    corr[0][3 * 128 :, :128] = slot_across
    corr[0][3 * 128 :, 128:] = slot_across

    places = (my_y, my_z)

    def block(line, k, c):
        return pl.ds(pl.multiple_of((line * RING + 2 * k + c) * SHARE, 16), SHARE)

    steps = [(i, line) for i in (2, 1, 3, 0) for line in range(2)]
    a_copies = [[], []]

    def send_a(p):
        first, width = PIECES[p]
        for n, (i, line) in enumerate(steps):
            k = lax.rem(places[line] + i, 4)
            a_send[p][n] = acc[block(line, k, 1 - my_c), first : first + width].astype(BF16)
            copy = pltpu.make_async_remote_copy(
                src_ref=a_send[p].at[n], dst_ref=a_recv[p].at[n],
                send_sem=a_send_sem.at[p, n], recv_sem=a_recv_sem.at[p, n],
                device_id={"sta": me + 1 - 2 * my_c}, device_id_type=MESH,
            )
            copy.start()
            a_copies[p].append(copy)

    for q in range(PARTS):
        width = WIDTHS[q]
        arrived = wr[q].at[pl.ds(0, MEMBERS - 1)]
        pltpu.make_async_copy(arrived, arrived, w_recv_sem.at[q]).wait()

        def repack(i, carry):
            both = wr[q][pl.ds(2 * i, 2)].astype(F32)
            rows = pl.ds(pl.multiple_of(i * 16, 16), 16)
            low = both[:, :8].reshape(16, width).astype(BF16)
            high = both[:, 8:].reshape(16, width).astype(BF16)
            for j in range(width // 128):
                wc[j, rows, :128] = low[:, j * 128 : (j + 1) * 128]
                wc[j, rows, 128:] = high[:, j * 128 : (j + 1) * 128]
            return carry

        lax.fori_loop(0, MEMBERS // 2, repack, 0)

        def correlate(pair, carry):
            for j in (2 * pair, 2 * pair + 1):
                real_at = pl.ds(pl.multiple_of(j * 128, 128), 128)
                imag_at = pl.ds(pl.multiple_of(WIDE + j * 128, 128), 128)
                for m in range(0, BLOCKS, 8):
                    both = jnp.dot(
                        sel[m : m + 8].reshape(8 * 2 * SHARE, STATIONS), wc[j], preferred_element_type=F32
                    )
                    for i in range(8 * SHARE // 16):
                        a0, a1 = both[i * 32 : i * 32 + 16, :128], both[i * 32 : i * 32 + 16, 128:]
                        b0, b1 = both[i * 32 + 16 : i * 32 + 32, :128], both[i * 32 + 16 : i * 32 + 32, 128:]
                        rows = slice(m * SHARE + i * 16, m * SHARE + i * 16 + 16)
                        cross[rows, real_at] = (a0 * b0 + a1 * b1).astype(BF16)
                        cross[rows, imag_at] = (a1 * b0 - a0 * b1).astype(BF16)
            return carry

        lax.fori_loop(0, width // 256, correlate, 0)

        bins = slice(STARTS[q], STARTS[q] + width)

        def add(columns, value):
            if q == 0:
                acc[:, columns] = value
            else:
                acc[:, columns] += value

        real, imag = cross.at[:, :width], cross.at[:, WIDE : WIDE + width]
        add(slice(896, COLS), jnp.dot(imag[...], tsin[bins, 128:], preferred_element_type=F32))
        if q == PARTS - 1:
            send_a(0)
        add(slice(0, 768), jnp.dot(real[...], tcos[bins, :768], preferred_element_type=F32))
        add(
            slice(768, 896),
            jnp.dot(real[...], tcos[bins, 768:], preferred_element_type=F32)
            + jnp.dot(imag[...], tsin[bins, :128], preferred_element_type=F32),
        )
        if q == PARTS - 1:
            send_a(1)

    b_copies = [[], []]
    for p, (first, width) in enumerate(PIECES):
        for n, (i, line) in enumerate(steps[:6]):
            k = lax.rem(places[line] + i, 4)
            a_copies[p][n].wait_recv()
            mine = acc[block(line, k, my_c), first : first + width]
            b_send[p][n] = (mine + a_recv[p][n].astype(F32)).astype(BF16)
            peer = row + 2 * k + my_c if line == 0 else k * RING + inside
            copy = pltpu.make_async_remote_copy(
                src_ref=b_send[p].at[n], dst_ref=b_recv[p].at[n],
                send_sem=b_send_sem.at[p, n], recv_sem=b_recv_sem.at[p, n],
                device_id={"sta": peer}, device_id_type=MESH,
            )
            copy.start()
            b_copies[p].append(copy)

    scale = F32(BINS ** (-0.5))
    owns = []
    for p, (first, width) in enumerate(PIECES):
        for line in range(2):
            a_copies[p][6 + line].wait_recv()
            for n in range(line, 6, 2):
                b_copies[p][n].wait_recv()
            total = acc[block(line, places[line], my_c), first : first + width]
            total = total + a_recv[p][6 + line].astype(F32)
            for n in range(line, 6, 2):
                total = total + b_recv[p][n].astype(F32)
            total = (total * scale).astype(BF16)
            for k in range(-(-width // SEG)):
                wide = min(SEG, width - k * SEG)
                at = k * 128 + line * SHARE
                corr[p][at : at + SHARE, :wide] = total[:, k * SEG : k * SEG + wide]

        def pack(t, carry):
            rows = pl.ds(pl.multiple_of(t * 256, 256), 256)
            out = jnp.dot(gsel[rows, :], corr[p][...], preferred_element_type=F32)
            c_send[p][pl.ds(t * 32, 32)] = out.reshape(32, 8, SEG).astype(BF16)
            return carry

        lax.fori_loop(0, DEVS // 32, pack, 0)
        own = pltpu.make_async_copy(c_send[p].at[dev], got[p].at[dev], own_sem.at[p])
        own.start()
        owns.append(own)

        def route(i, carry):
            peer = lax.rem(dev + i * 53, DEVS)
            pltpu.make_async_remote_copy(
                src_ref=c_send[p].at[peer], dst_ref=got[p].at[dev],
                send_sem=c_send_sem.at[p], recv_sem=c_recv_sem.at[p],
                device_id={"grp": peer // MEMBERS, "sta": lax.rem(peer, MEMBERS)},
                device_id_type=MESH,
            ).start()
            return carry

        lax.fori_loop(1, DEVS, route, 0)

    for p in range(2):
        for copy in a_copies[p]:
            copy.wait_send()
        for copy in b_copies[p]:
            copy.wait_send()
    pltpu.make_async_copy(known, known, id_send_sem).wait()
    for q in range(PARTS):
        sent = wr[q].at[pl.ds(0, MEMBERS - 1)]
        pltpu.make_async_copy(sent, sent, w_send_sem.at[q]).wait()
    for p in range(2):
        owns[p].wait()
        rest = c_send[p].at[pl.ds(0, DEVS - 1)]
        pltpu.make_async_copy(rest, rest, c_send_sem.at[p]).wait()
        pltpu.make_async_copy(rest, rest, c_recv_sem.at[p]).wait()


def correlate_and_route(*operands):
    vmem = pl.BlockSpec(memory_space=pltpu.VMEM)
    dma = pltpu.SemaphoreType.DMA
    return pl.pallas_call(
        main_kernel,
        out_shape=[jax.ShapeDtypeStruct((DEVS, 8, SEG), BF16)] * 2,
        in_specs=[pl.BlockSpec(memory_space=pltpu.HBM), vmem],
        out_specs=[pl.BlockSpec(memory_space=pl.ANY)] * 2,
        scratch_shapes=[
            *[pltpu.VMEM((RING, 16, w), BF16) for w in WIDTHS],
            *[pltpu.VMEM((MEMBERS, 16, w), BF16) for w in WIDTHS],
            pltpu.VMEM((RING, 2, BINS), F32),
            pltpu.VMEM((WIDE // 128, STATIONS, 256), BF16),
            pltpu.VMEM((BLOCKS, 8, 128), jnp.int32),
            pltpu.VMEM((BLOCKS, 2 * SHARE, STATIONS), BF16),
            pltpu.VMEM((SLAB, 896), BF16),
            pltpu.VMEM((SLAB, 896), BF16),
            pltpu.VMEM((RING * PAIRS, COLS), F32),
            pltpu.VMEM((RING * PAIRS, 2 * WIDE), BF16),
            *[pltpu.VMEM((8, SHARE, w), BF16) for _ in range(2) for _, w in PIECES],
            *[pltpu.VMEM((6, SHARE, w), BF16) for _ in range(2) for _, w in PIECES],
            *[pltpu.VMEM((SEGS * 128, SEG), BF16) for _ in range(2)],
            pltpu.VMEM((DEVS * 8, SEGS * 128), BF16),
            *[pltpu.VMEM((DEVS, 8, SEG), BF16) for _ in range(2)],
            dma, dma,
            dma((PARTS,)), dma((PARTS,)),
            dma((2, 8)), dma((2, 8)),
            dma((2, 6)), dma((2, 6)),
            dma((2,)), dma((2,)), dma((2,)), dma((RING,)),
        ],
        compiler_params=pltpu.CompilerParams(
            collective_id=0, has_side_effects=True, vmem_limit_bytes=52 * 1024 * 1024
        ),
    )(*operands)


def stack_kernel(got_a, got_b, stacks_ref, out_ref):
    rows = DEVS * 8
    got = [ref[...].reshape(rows, SEG) for ref in (got_a, got_b)]
    first = jnp.where(lax.broadcasted_iota(jnp.int32, (8, SEG), 1) == 0, F32(1), F32(0)).astype(BF16)
    marks = lax.dot_general(first, got[0], (((1,), (1,)), ((), ())), preferred_element_type=F32)
    place = lax.broadcasted_iota(jnp.int32, (8, rows), 1) & 3
    marks = jnp.where(place == 3, marks, F32(0))
    marks = jnp.maximum(marks, pltpu.roll(marks, rows - 1, 1))
    marks = jnp.maximum(marks, pltpu.roll(marks, rows - 2, 1))
    code = (marks.astype(jnp.int32) + place * PAIRS)[0:1]
    want = lax.broadcasted_iota(jnp.int32, (SEGS * PAIRS, rows), 0)
    hot = jnp.where(want == code, F32(1), F32(0)).astype(BF16)
    near, far = [jnp.dot(hot, g, preferred_element_type=F32) for g in (got[1], got[0])]
    parts = [near[k * PAIRS : (k + 1) * PAIRS] for k in range(SEGS)]
    parts += [far[k * PAIRS : (k + 1) * PAIRS] for k in range(SEGS - 1)]
    sums = jnp.concatenate(parts, axis=1)
    even, odd = sums[:, :896], sums[:, SIDE : SIDE + 896]
    tiles = 7
    gap = even - odd
    high = gap.astype(BF16)
    low = (gap - high.astype(F32)).astype(BF16)
    stack = jnp.concatenate(
        [v[:, t * 128 : (t + 1) * 128] for v in (high, low) for t in range(tiles)], axis=0
    )
    mirror = lax.broadcasted_iota(jnp.int32, (128, 128), 0) + lax.broadcasted_iota(jnp.int32, (128, 128), 1)
    mirror = jnp.where(mirror == 127, F32(1), F32(0)).astype(BF16)
    turned = jnp.dot(stack, mirror, preferred_element_type=F32)
    turned = turned[: tiles * PAIRS] + turned[tiles * PAIRS :]
    behind = jnp.concatenate(
        [turned[t * PAIRS : (t + 1) * PAIRS] for t in reversed(range(tiles))], axis=1
    )
    skip = tiles * 128 - HALF
    out_ref[:, :HALF] = stacks_ref[:, :HALF] + behind[:, skip:]
    out_ref[:, HALF:] = stacks_ref[:, HALF:] + (even + odd)[:, 1:HALF]


def add_rows(got_a, got_b, stacks):
    vmem = pl.BlockSpec(memory_space=pltpu.VMEM)
    return pl.pallas_call(
        stack_kernel,
        out_shape=jax.ShapeDtypeStruct(stacks.shape, F32),
        in_specs=[vmem] * 3,
        out_specs=vmem,
        compiler_params=pltpu.CompilerParams(vmem_limit_bytes=40 * 1024 * 1024),
    )(got_a, got_b, stacks)


def local(spectra, stacks, pair_sta, pair_valid, owner, slot):
    rows = [pair_sta, pair_valid[None, :], owner.reshape(1, PAIRS), slot[None, :]]
    meta = jnp.pad(jnp.concatenate(rows, axis=0), ((0, 3), (0, 128 - PAIRS)))
    got_a, got_b = correlate_and_route(spectra, meta)
    return add_rows(got_a, got_b, stacks)


def solution(mesh):
    return jax.shard_map(
        local,
        mesh=mesh,
        in_specs=(
            P(("grp", "sta"), None, None),
            P(("grp", "sta"), None),
            P(None, ("grp", "sta")),
            P(("grp", "sta")),
            P(("grp", "sta"), None),
            P(("grp", "sta")),
        ),
        out_specs=P(("grp", "sta"), None),
        check_vma=False,
    )
```

```python
import functools
import math

import jax
import jax.numpy as jnp
from jax import lax
from jax.experimental import pallas as pl
from jax.experimental.pallas import tpu as pltpu
from jax.sharding import PartitionSpec as P

BAND = 64
MESH = pl.DeviceIdType.MESH
BF16 = jnp.bfloat16
F32 = jnp.float32

BINS = 18432
LAGS = 1601
HALF = (LAGS + 1) // 2
SIDE = 832
COLS = 2 * SIDE
PAIRS = 96
SHARE = PAIRS // 2
RING = 8
BLOCKS = 2 * RING
SLAB = BINS // RING
WIDTHS = (512, 512, 512, 512, 256)
STARTS = (0, 512, 1024, 1536, 2048)
WIDE = max(WIDTHS)
PARTS = len(WIDTHS)
MEMBERS = 32
GROUPS = 4
DEVS = 128
STATIONS = 256
SEG = 256
SEGS = 4
PIECES = ((1024, 640), (0, 1024))


def angles(freqs, shifts):
    product = (freqs * shifts).astype(F32)
    turns = jnp.floor(product * F32(1.0 / (2 * BINS)))
    return (product - turns * F32(2 * BINS)) * F32(math.pi / BINS)


def main_kernel(spectra_ref, meta_ref, got_a, got_b, *scratch):
    ws, wr = scratch[:PARTS], scratch[PARTS : 2 * PARTS]
    (
        x_ref, wc, ids_all, sel, tcos, tsin, acc, cross,
        a_send_0, a_send_1, a_recv_0, a_recv_1, b_send_0, b_send_1, b_recv_0, b_recv_1,
        corr_0, corr_1, gsel, c_send_0, c_send_1,
        id_send_sem, id_recv_sem, w_send_sem, w_recv_sem,
        a_send_sem, a_recv_sem, b_send_sem, b_recv_sem, c_send_sem, c_recv_sem, own_sem, x_sem,
    ) = scratch[2 * PARTS :]
    a_send, a_recv = (a_send_0, a_send_1), (a_recv_0, a_recv_1)
    b_send, b_recv = (b_send_0, b_send_1), (b_recv_0, b_recv_1)
    corr, c_send, got = (corr_0, corr_1), (c_send_0, c_send_1), (got_a, got_b)
    grp = lax.axis_index("grp")
    me = lax.axis_index("sta")
    dev = grp * MEMBERS + me
    my_z, inside = me // RING, lax.rem(me, RING)
    my_y, my_c = inside // 2, lax.rem(inside, 2)

    def slab_of(member):
        z, rest = member // RING, lax.rem(member, RING)
        return 2 * lax.rem(z + rest // 2, 4) + lax.rem(rest, 2)

    my_slab = slab_of(me)
    row = me - inside

    def load(s):
        bins = pl.ds(pl.multiple_of(s * SLAB, 128), SLAB)
        return pltpu.make_async_copy(spectra_ref.at[:, :, bins], x_ref.at[:, :, bins], x_sem.at[s])

    for s in range(RING):
        load(s).start()

    barrier = pltpu.get_barrier_semaphore()

    def greet(i, carry):
        pl.semaphore_signal(
            barrier, inc=1, device_id={"grp": grp, "sta": lax.rem(me + i, MEMBERS)}, device_id_type=MESH
        )
        return carry

    def greet_across(i, carry):
        pl.semaphore_signal(
            barrier, inc=1, device_id={"grp": lax.rem(grp + i, GROUPS), "sta": me}, device_id_type=MESH
        )
        return carry

    lax.fori_loop(1, GROUPS, greet_across, 0)
    lax.fori_loop(1, MEMBERS, greet, 0)

    lane = lax.broadcasted_iota(jnp.int32, (128, 128), 1) // BAND
    sub = lax.broadcasted_iota(jnp.int32, (128, 128), 0) // BAND
    bands = jnp.where(lane == sub, F32(1), F32(0))

    def whiten(s, carry):
        load(s).wait()
        base = pl.multiple_of(s * SLAB, 128)
        x0 = x_ref[:, 0, pl.ds(base, SLAB)]
        x1 = x_ref[:, 1, pl.ds(base, SLAB)]
        square = x0 * x0 + x1 * x1
        tiles = SLAB // 128
        rows = jnp.concatenate([square[:, j * 128 : (j + 1) * 128] for j in range(tiles)], axis=0)
        power = jnp.dot(
            rows, bands, precision=lax.Precision.HIGHEST, preferred_element_type=F32
        ) * F32(1.0 / (2 * BAND))
        inverse = lax.rsqrt(power + F32(1e-06))
        for j in range(tiles):
            inv = inverse[j * 8 : (j + 1) * 8]
            cut = slice(j * 128, (j + 1) * 128)
            both = jnp.concatenate([x0[:, cut] * inv, x1[:, cut] * inv], axis=0).astype(BF16)
            q = max(p for p in range(PARTS) if STARTS[p] <= j * 128)
            o = j * 128 - STARTS[q]
            ws[q][s, :, o : o + 128] = both
        return carry

    lax.fori_loop(0, RING, whiten, 0)
    pl.semaphore_wait(barrier, GROUPS - 1 + MEMBERS - 1)

    def send_ids(slot, peer):
        pltpu.make_async_remote_copy(
            src_ref=meta_ref, dst_ref=ids_all.at[slot],
            send_sem=id_send_sem, recv_sem=id_recv_sem,
            device_id={"sta": peer}, device_id_type=MESH,
        ).start()

    def along_y(i, carry):
        send_ids(inside, row + lax.rem(inside + i, RING))
        return carry

    def along_z(i, carry):
        send_ids(RING + 2 * my_z + my_c, lax.rem(my_z + 1 + i // 2, 4) * RING + 2 * my_y + lax.rem(i, 2))
        return carry

    lax.fori_loop(1, RING, along_y, 0)
    lax.fori_loop(0, 6, along_z, 0)
    ids_all[inside] = meta_ref[...]
    ids_all[RING + 2 * my_z + my_c] = meta_ref[...]

    def send_part(q):
        def one(i, carry):
            peer = lax.rem(me + i * 11, MEMBERS)
            pltpu.make_async_remote_copy(
                src_ref=ws[q].at[slab_of(peer)], dst_ref=wr[q].at[me],
                send_sem=w_send_sem.at[q], recv_sem=w_recv_sem.at[q],
                device_id={"sta": peer}, device_id_type=MESH,
            ).start()
            return carry

        lax.fori_loop(1, MEMBERS, one, 0)
        wr[q][me] = ws[q][my_slab]

    for q in range(PARTS):
        send_part(q)

    start = my_slab * SLAB

    def table_column(cb, half):
        column = lax.broadcasted_iota(jnp.int32, (64, 128), 1) + cb * 128
        cosine_side = column < SIDE
        lags = jnp.where(cosine_side, column, column - SIDE)
        freqs = lax.broadcasted_iota(jnp.int32, (64, 128), 0) + start
        theta = angles(freqs, lags)
        cosines, sines = jnp.cos(theta), jnp.sin(theta)
        turn = angles(jnp.full((8, 128), 64, jnp.int32), lags[:8])
        tc = jnp.concatenate([jnp.cos(turn)] * 8, axis=0)
        ts = jnp.concatenate([jnp.sin(turn)] * 8, axis=0)

        def rotate(i, state):
            c, s = state
            for step in range(4):
                rows = pl.ds(pl.multiple_of(i * 256 + step * 64, 64), 64)
                if half == "both":
                    tcos[rows, SIDE - 64 : SIDE + 64] = jnp.where(cosine_side, c, F32(0)).astype(BF16)
                    tsin[rows, :128] = jnp.where(cosine_side, F32(0), -s).astype(BF16)
                elif half == "cos":
                    tcos[rows, pl.ds(pl.multiple_of(cb * 128, 128), 128)] = c.astype(BF16)
                else:
                    tsin[rows, pl.ds(pl.multiple_of(cb * 128 - 768, 128), 128)] = (-s).astype(BF16)
                c, s = c * tc - s * ts, s * tc + c * ts
            return c, s

        lax.fori_loop(0, SLAB // 256, rotate, (cosines, sines))

    def cosine_column(cb, carry):
        table_column(cb, "cos")
        return carry

    def sine_column(cb, carry):
        table_column(cb, "sin")
        return carry

    lax.fori_loop(0, 6, cosine_column, 0)
    table_column(6, "both")
    lax.fori_loop(7, 13, sine_column, 0)

    known = ids_all.at[pl.ds(0, 13)]
    pltpu.make_async_copy(known, known, id_recv_sem).wait()
    ids_all[RING + 2 * my_z + 1 - my_c] = ids_all[2 * my_y + 1 - my_c]

    def choose(m, carry):
        station = lax.broadcasted_iota(jnp.int32, (STATIONS, 128), 0)
        for line in range(2):
            for side in range(2):
                wanted = ids_all[line * RING + m, side : side + 1, :]
                hot = jnp.transpose(jnp.where(station == wanted, F32(1), F32(0))).astype(BF16)
                for i in range(SHARE // 16):
                    at, pair = i * 32 + side * 16, line * SHARE + i * 16
                    sel[line * RING + m, at : at + 16, :] = hot[pair : pair + 16]
        return carry

    lax.fori_loop(0, RING, choose, 0)

    meta = meta_ref[...]
    square = (128, 128)
    sub, lane = lax.broadcasted_iota(jnp.int32, square, 0), lax.broadcasted_iota(jnp.int32, square, 1)
    dest = meta[3:4, :]
    dest_across = jnp.transpose(jnp.broadcast_to(dest.astype(F32), square)).astype(jnp.int32)
    earlier = (dest_across == dest) & (sub < lane) & (sub < PAIRS)
    position = jnp.sum(jnp.where(earlier, F32(1), F32(0)), axis=0, keepdims=True).astype(jnp.int32)
    counted = (lane[0:1] < PAIRS) & (meta[2:3, :] == 1)
    code = jnp.where(counted, dest * 8 + position * SEGS, -64)

    def place(t, carry):
        target = lax.broadcasted_iota(jnp.int32, (128, 128), 0) + t * 128
        rows = pl.ds(pl.multiple_of(t * 128, 128), 128)
        for k in range(SEGS):
            gsel[rows, k * 128 : (k + 1) * 128] = jnp.where(target == code + k, F32(1), F32(0)).astype(BF16)
        return carry

    lax.fori_loop(0, DEVS * 8 // 128, place, 0)
    slot_across = jnp.transpose(jnp.broadcast_to(meta[4:5, :].astype(F32), square)).astype(BF16)
    for p in range(2):
        corr[p][...] = jnp.zeros_like(corr[p])
    corr[0][3 * 128 :, :128] = slot_across
    corr[0][3 * 128 :, 128:] = slot_across

    places = (my_y, my_z)

    def block(line, k, c):
        return pl.ds(pl.multiple_of((line * RING + 2 * k + c) * SHARE, 16), SHARE)

    steps = [(i, line) for i in (2, 1, 3, 0) for line in range(2)]
    a_copies = [[], []]

    def send_a(p):
        first, width = PIECES[p]
        for n, (i, line) in enumerate(steps):
            k = lax.rem(places[line] + i, 4)
            a_send[p][n] = acc[block(line, k, 1 - my_c), first : first + width].astype(BF16)
            copy = pltpu.make_async_remote_copy(
                src_ref=a_send[p].at[n], dst_ref=a_recv[p].at[n],
                send_sem=a_send_sem.at[p, n], recv_sem=a_recv_sem.at[p, n],
                device_id={"sta": me + 1 - 2 * my_c}, device_id_type=MESH,
            )
            copy.start()
            a_copies[p].append(copy)

    for q in range(PARTS):
        width = WIDTHS[q]
        arrived = wr[q].at[pl.ds(0, MEMBERS - 1)]
        pltpu.make_async_copy(arrived, arrived, w_recv_sem.at[q]).wait()

        def repack(i, carry):
            both = wr[q][pl.ds(2 * i, 2)].astype(F32)
            rows = pl.ds(pl.multiple_of(i * 16, 16), 16)
            low = both[:, :8].reshape(16, width).astype(BF16)
            high = both[:, 8:].reshape(16, width).astype(BF16)
            for j in range(width // 128):
                wc[j, rows, :128] = low[:, j * 128 : (j + 1) * 128]
                wc[j, rows, 128:] = high[:, j * 128 : (j + 1) * 128]
            return carry

        lax.fori_loop(0, MEMBERS // 2, repack, 0)

        def correlate(pair, carry):
            for j in (2 * pair, 2 * pair + 1):
                real_at = pl.ds(pl.multiple_of(j * 128, 128), 128)
                imag_at = pl.ds(pl.multiple_of(WIDE + j * 128, 128), 128)
                for m in range(0, BLOCKS, 8):
                    both = jnp.dot(
                        sel[m : m + 8].reshape(8 * 2 * SHARE, STATIONS), wc[j], preferred_element_type=F32
                    )
                    for i in range(8 * SHARE // 16):
                        a0, a1 = both[i * 32 : i * 32 + 16, :128], both[i * 32 : i * 32 + 16, 128:]
                        b0, b1 = both[i * 32 + 16 : i * 32 + 32, :128], both[i * 32 + 16 : i * 32 + 32, 128:]
                        rows = slice(m * SHARE + i * 16, m * SHARE + i * 16 + 16)
                        cross[rows, real_at] = (a0 * b0 + a1 * b1).astype(BF16)
                        cross[rows, imag_at] = (a1 * b0 - a0 * b1).astype(BF16)
            return carry

        lax.fori_loop(0, width // 256, correlate, 0)

        bins = slice(STARTS[q], STARTS[q] + width)

        def add(columns, value):
            if q == 0:
                acc[:, columns] = value
            else:
                acc[:, columns] += value

        real, imag = cross.at[:, :width], cross.at[:, WIDE : WIDE + width]
        add(slice(896, COLS), jnp.dot(imag[...], tsin[bins, 128:], preferred_element_type=F32))
        if q == PARTS - 1:
            send_a(0)
        add(slice(0, 768), jnp.dot(real[...], tcos[bins, :768], preferred_element_type=F32))
        add(
            slice(768, 896),
            jnp.dot(real[...], tcos[bins, 768:], preferred_element_type=F32)
            + jnp.dot(imag[...], tsin[bins, :128], preferred_element_type=F32),
        )
        if q == PARTS - 1:
            send_a(1)

    b_copies = [[], []]
    for p, (first, width) in enumerate(PIECES):
        for n, (i, line) in enumerate(steps[:6]):
            k = lax.rem(places[line] + i, 4)
            a_copies[p][n].wait_recv()
            mine = acc[block(line, k, my_c), first : first + width]
            b_send[p][n] = (mine + a_recv[p][n].astype(F32)).astype(BF16)
            peer = row + 2 * k + my_c if line == 0 else k * RING + inside
            copy = pltpu.make_async_remote_copy(
                src_ref=b_send[p].at[n], dst_ref=b_recv[p].at[n],
                send_sem=b_send_sem.at[p, n], recv_sem=b_recv_sem.at[p, n],
                device_id={"sta": peer}, device_id_type=MESH,
            )
            copy.start()
            b_copies[p].append(copy)

    scale = F32(BINS ** (-0.5))
    owns = []
    for p, (first, width) in enumerate(PIECES):
        for line in range(2):
            a_copies[p][6 + line].wait_recv()
            for n in range(line, 6, 2):
                b_copies[p][n].wait_recv()
            total = acc[block(line, places[line], my_c), first : first + width]
            total = total + a_recv[p][6 + line].astype(F32)
            for n in range(line, 6, 2):
                total = total + b_recv[p][n].astype(F32)
            total = (total * scale).astype(BF16)
            for k in range(-(-width // SEG)):
                wide = min(SEG, width - k * SEG)
                at = k * 128 + line * SHARE
                corr[p][at : at + SHARE, :wide] = total[:, k * SEG : k * SEG + wide]

        def pack(t, carry):
            rows = pl.ds(pl.multiple_of(t * 256, 256), 256)
            out = jnp.dot(gsel[rows, :], corr[p][...], preferred_element_type=F32)
            c_send[p][pl.ds(t * 32, 32)] = out.reshape(32, 8, SEG).astype(BF16)
            return carry

        lax.fori_loop(0, DEVS // 32, pack, 0)
        own = pltpu.make_async_copy(c_send[p].at[dev], got[p].at[dev], own_sem.at[p])
        own.start()
        owns.append(own)

        def route(i, carry):
            peer = lax.rem(dev + i * 53, DEVS)
            pltpu.make_async_remote_copy(
                src_ref=c_send[p].at[peer], dst_ref=got[p].at[dev],
                send_sem=c_send_sem.at[p], recv_sem=c_recv_sem.at[p],
                device_id={"grp": peer // MEMBERS, "sta": lax.rem(peer, MEMBERS)},
                device_id_type=MESH,
            ).start()
            return carry

        lax.fori_loop(1, DEVS, route, 0)

    for p in range(2):
        for copy in a_copies[p]:
            copy.wait_send()
        for copy in b_copies[p]:
            copy.wait_send()
    pltpu.make_async_copy(known, known, id_send_sem).wait()
    for q in range(PARTS):
        sent = wr[q].at[pl.ds(0, MEMBERS - 1)]
        pltpu.make_async_copy(sent, sent, w_send_sem.at[q]).wait()
    for p in range(2):
        owns[p].wait()
        rest = c_send[p].at[pl.ds(0, DEVS - 1)]
        pltpu.make_async_copy(rest, rest, c_send_sem.at[p]).wait()
        pltpu.make_async_copy(rest, rest, c_recv_sem.at[p]).wait()


def correlate_and_route(*operands):
    vmem = pl.BlockSpec(memory_space=pltpu.VMEM)
    dma = pltpu.SemaphoreType.DMA
    return pl.pallas_call(
        main_kernel,
        out_shape=[jax.ShapeDtypeStruct((DEVS, 8, SEG), BF16)] * 2,
        in_specs=[pl.BlockSpec(memory_space=pltpu.HBM), vmem],
        out_specs=[pl.BlockSpec(memory_space=pl.ANY)] * 2,
        scratch_shapes=[
            *[pltpu.VMEM((RING, 16, w), BF16) for w in WIDTHS],
            *[pltpu.VMEM((MEMBERS, 16, w), BF16) for w in WIDTHS],
            pltpu.VMEM((RING, 2, BINS), F32),
            pltpu.VMEM((WIDE // 128, STATIONS, 256), BF16),
            pltpu.VMEM((BLOCKS, 8, 128), jnp.int32),
            pltpu.VMEM((BLOCKS, 2 * SHARE, STATIONS), BF16),
            pltpu.VMEM((SLAB, 896), BF16),
            pltpu.VMEM((SLAB, 896), BF16),
            pltpu.VMEM((RING * PAIRS, COLS), F32),
            pltpu.VMEM((RING * PAIRS, 2 * WIDE), BF16),
            *[pltpu.VMEM((8, SHARE, w), BF16) for _ in range(2) for _, w in PIECES],
            *[pltpu.VMEM((6, SHARE, w), BF16) for _ in range(2) for _, w in PIECES],
            *[pltpu.VMEM((SEGS * 128, SEG), BF16) for _ in range(2)],
            pltpu.VMEM((DEVS * 8, SEGS * 128), BF16),
            *[pltpu.VMEM((DEVS, 8, SEG), BF16) for _ in range(2)],
            dma, dma,
            dma((PARTS,)), dma((PARTS,)),
            dma((2, 8)), dma((2, 8)),
            dma((2, 6)), dma((2, 6)),
            dma((2,)), dma((2,)), dma((2,)), dma((RING,)),
        ],
        compiler_params=pltpu.CompilerParams(
            collective_id=0, has_side_effects=True, vmem_limit_bytes=52 * 1024 * 1024
        ),
    )(*operands)


def stack_kernel(got_a, got_b, stacks_ref, out_ref):
    rows = DEVS * 8
    got = [ref[...].reshape(rows, SEG) for ref in (got_a, got_b)]
    first = jnp.where(lax.broadcasted_iota(jnp.int32, (8, SEG), 1) == 0, F32(1), F32(0)).astype(BF16)
    marks = lax.dot_general(first, got[0], (((1,), (1,)), ((), ())), preferred_element_type=F32)
    place = lax.broadcasted_iota(jnp.int32, (8, rows), 1) & 3
    marks = jnp.where(place == 3, marks, F32(0))
    marks = jnp.maximum(marks, pltpu.roll(marks, rows - 1, 1))
    marks = jnp.maximum(marks, pltpu.roll(marks, rows - 2, 1))
    code = (marks.astype(jnp.int32) + place * PAIRS)[0:1]
    want = lax.broadcasted_iota(jnp.int32, (SEGS * PAIRS, rows), 0)
    hot = jnp.where(want == code, F32(1), F32(0)).astype(BF16)
    near, far = [jnp.dot(hot, g, preferred_element_type=F32) for g in (got[1], got[0])]
    parts = [near[k * PAIRS : (k + 1) * PAIRS] for k in range(SEGS)]
    parts += [far[k * PAIRS : (k + 1) * PAIRS] for k in range(SEGS - 1)]
    sums = jnp.concatenate(parts, axis=1)
    even, odd = sums[:, :896], sums[:, SIDE : SIDE + 896]
    tiles = 7
    gap = even - odd
    high = gap.astype(BF16)
    low = (gap - high.astype(F32)).astype(BF16)
    stack = jnp.concatenate(
        [v[:, t * 128 : (t + 1) * 128] for v in (high, low) for t in range(tiles)], axis=0
    )
    mirror = lax.broadcasted_iota(jnp.int32, (128, 128), 0) + lax.broadcasted_iota(jnp.int32, (128, 128), 1)
    mirror = jnp.where(mirror == 127, F32(1), F32(0)).astype(BF16)
    turned = jnp.dot(stack, mirror, preferred_element_type=F32)
    turned = turned[: tiles * PAIRS] + turned[tiles * PAIRS :]
    behind = jnp.concatenate(
        [turned[t * PAIRS : (t + 1) * PAIRS] for t in reversed(range(tiles))], axis=1
    )
    skip = tiles * 128 - HALF
    out_ref[:, :HALF] = stacks_ref[:, :HALF] + behind[:, skip:]
    out_ref[:, HALF:] = stacks_ref[:, HALF:] + (even + odd)[:, 1:HALF]


def add_rows(got_a, got_b, stacks):
    vmem = pl.BlockSpec(memory_space=pltpu.VMEM)
    return pl.pallas_call(
        stack_kernel,
        out_shape=jax.ShapeDtypeStruct(stacks.shape, F32),
        in_specs=[vmem] * 3,
        out_specs=vmem,
        compiler_params=pltpu.CompilerParams(vmem_limit_bytes=40 * 1024 * 1024),
    )(got_a, got_b, stacks)


def local(spectra, stacks, pair_sta, pair_valid, owner, slot):
    rows = [pair_sta, pair_valid[None, :], owner.reshape(1, PAIRS), slot[None, :]]
    meta = jnp.pad(jnp.concatenate(rows, axis=0), ((0, 3), (0, 128 - PAIRS)))
    got_a, got_b = correlate_and_route(spectra, meta)
    return add_rows(got_a, got_b, stacks)


def solution(mesh):
    return jax.shard_map(
        local,
        mesh=mesh,
        in_specs=(
            P(("grp", "sta"), None, None),
            P(("grp", "sta"), None),
            P(None, ("grp", "sta")),
            P(("grp", "sta")),
            P(("grp", "sta"), None),
            P(("grp", "sta")),
        ),
        out_specs=P(("grp", "sta"), None),
        check_vma=False,
    )
```

```python
import functools
import math

import jax
import jax.numpy as jnp
from jax import lax
from jax.experimental import pallas as pl
from jax.experimental.pallas import tpu as pltpu
from jax.sharding import PartitionSpec as P

BAND = 64
MESH = pl.DeviceIdType.MESH
BF16 = jnp.bfloat16
F32 = jnp.float32

BINS = 18432
LAGS = 1601
HALF = (LAGS + 1) // 2
SIDE = 832
COLS = 2 * SIDE
PAIRS = 96
SHARE = PAIRS // 2
RING = 8
BLOCKS = 2 * RING
SLAB = BINS // RING
WIDTHS = (512, 512, 512, 512, 256)
STARTS = (0, 512, 1024, 1536, 2048)
WIDE = max(WIDTHS)
PARTS = len(WIDTHS)
MEMBERS = 32
GROUPS = 4
DEVS = 128
STATIONS = 256
SEG = 256
SEGS = 4
PIECES = ((1024, 640), (0, 1024))


def angles(freqs, shifts):
    product = (freqs * shifts).astype(F32)
    turns = jnp.floor(product * F32(1.0 / (2 * BINS)))
    return (product - turns * F32(2 * BINS)) * F32(math.pi / BINS)


def main_kernel(spectra_ref, meta_ref, got_a, got_b, *scratch):
    ws, wr = scratch[:PARTS], scratch[PARTS : 2 * PARTS]
    (
        x_ref, wc, ids_all, sel, tcos, tsin, acc, cross,
        a_send_0, a_send_1, a_recv_0, a_recv_1, b_send_0, b_send_1, b_recv_0, b_recv_1,
        corr_0, corr_1, gsel, c_send_0, c_send_1,
        id_send_sem, id_recv_sem, w_send_sem, w_recv_sem,
        a_send_sem, a_recv_sem, b_send_sem, b_recv_sem, c_send_sem, c_recv_sem, own_sem, x_sem,
    ) = scratch[2 * PARTS :]
    a_send, a_recv = (a_send_0, a_send_1), (a_recv_0, a_recv_1)
    b_send, b_recv = (b_send_0, b_send_1), (b_recv_0, b_recv_1)
    corr, c_send, got = (corr_0, corr_1), (c_send_0, c_send_1), (got_a, got_b)
    grp = lax.axis_index("grp")
    me = lax.axis_index("sta")
    dev = grp * MEMBERS + me
    my_z, inside = me // RING, lax.rem(me, RING)
    my_y, my_c = inside // 2, lax.rem(inside, 2)

    def slab_of(member):
        z, rest = member // RING, lax.rem(member, RING)
        return 2 * lax.rem(z + rest // 2, 4) + lax.rem(rest, 2)

    my_slab = slab_of(me)
    row = me - inside

    def load(s):
        bins = pl.ds(pl.multiple_of(s * SLAB, 128), SLAB)
        return pltpu.make_async_copy(spectra_ref.at[:, :, bins], x_ref.at[:, :, bins], x_sem.at[s])

    for s in range(RING):
        load(s).start()

    barrier = pltpu.get_barrier_semaphore()

    def greet(i, carry):
        pl.semaphore_signal(
            barrier, inc=1, device_id={"grp": grp, "sta": lax.rem(me + i, MEMBERS)}, device_id_type=MESH
        )
        return carry

    def greet_across(i, carry):
        pl.semaphore_signal(
            barrier, inc=1, device_id={"grp": lax.rem(grp + i, GROUPS), "sta": me}, device_id_type=MESH
        )
        return carry

    lax.fori_loop(1, GROUPS, greet_across, 0)
    lax.fori_loop(1, MEMBERS, greet, 0)

    lane = lax.broadcasted_iota(jnp.int32, (128, 128), 1) // BAND
    sub = lax.broadcasted_iota(jnp.int32, (128, 128), 0) // BAND
    bands = jnp.where(lane == sub, F32(1), F32(0))

    def whiten(s, carry):
        load(s).wait()
        base = pl.multiple_of(s * SLAB, 128)
        x0 = x_ref[:, 0, pl.ds(base, SLAB)]
        x1 = x_ref[:, 1, pl.ds(base, SLAB)]
        square = x0 * x0 + x1 * x1
        tiles = SLAB // 128
        rows = jnp.concatenate([square[:, j * 128 : (j + 1) * 128] for j in range(tiles)], axis=0)
        power = jnp.dot(
            rows, bands, precision=lax.Precision.HIGHEST, preferred_element_type=F32
        ) * F32(1.0 / (2 * BAND))
        inverse = lax.rsqrt(power + F32(1e-06))
        for j in range(tiles):
            inv = inverse[j * 8 : (j + 1) * 8]
            cut = slice(j * 128, (j + 1) * 128)
            both = jnp.concatenate([x0[:, cut] * inv, x1[:, cut] * inv], axis=0).astype(BF16)
            q = max(p for p in range(PARTS) if STARTS[p] <= j * 128)
            o = j * 128 - STARTS[q]
            ws[q][s, :, o : o + 128] = both
        return carry

    lax.fori_loop(0, RING, whiten, 0)
    pl.semaphore_wait(barrier, GROUPS - 1 + MEMBERS - 1)

    def send_ids(slot, peer):
        pltpu.make_async_remote_copy(
            src_ref=meta_ref, dst_ref=ids_all.at[slot],
            send_sem=id_send_sem, recv_sem=id_recv_sem,
            device_id={"sta": peer}, device_id_type=MESH,
        ).start()

    def along_y(i, carry):
        send_ids(inside, row + lax.rem(inside + i, RING))
        return carry

    def along_z(i, carry):
        send_ids(RING + 2 * my_z + my_c, lax.rem(my_z + 1 + i // 2, 4) * RING + 2 * my_y + lax.rem(i, 2))
        return carry

    lax.fori_loop(1, RING, along_y, 0)
    lax.fori_loop(0, 6, along_z, 0)
    ids_all[inside] = meta_ref[...]
    ids_all[RING + 2 * my_z + my_c] = meta_ref[...]

    def send_part(q):
        def one(i, carry):
            peer = lax.rem(me + i * 11, MEMBERS)
            pltpu.make_async_remote_copy(
                src_ref=ws[q].at[slab_of(peer)], dst_ref=wr[q].at[me],
                send_sem=w_send_sem.at[q], recv_sem=w_recv_sem.at[q],
                device_id={"sta": peer}, device_id_type=MESH,
            ).start()
            return carry

        lax.fori_loop(1, MEMBERS, one, 0)
        wr[q][me] = ws[q][my_slab]

    for q in range(PARTS):
        send_part(q)

    start = my_slab * SLAB

    def table_column(cb, half):
        column = lax.broadcasted_iota(jnp.int32, (64, 128), 1) + cb * 128
        cosine_side = column < SIDE
        lags = jnp.where(cosine_side, column, column - SIDE)
        freqs = lax.broadcasted_iota(jnp.int32, (64, 128), 0) + start
        theta = angles(freqs, lags)
        cosines, sines = jnp.cos(theta), jnp.sin(theta)
        turn = angles(jnp.full((8, 128), 64, jnp.int32), lags[:8])
        tc = jnp.concatenate([jnp.cos(turn)] * 8, axis=0)
        ts = jnp.concatenate([jnp.sin(turn)] * 8, axis=0)

        def rotate(i, state):
            c, s = state
            for step in range(4):
                rows = pl.ds(pl.multiple_of(i * 256 + step * 64, 64), 64)
                if half == "both":
                    tcos[rows, SIDE - 64 : SIDE + 64] = jnp.where(cosine_side, c, F32(0)).astype(BF16)
                    tsin[rows, :128] = jnp.where(cosine_side, F32(0), -s).astype(BF16)
                elif half == "cos":
                    tcos[rows, pl.ds(pl.multiple_of(cb * 128, 128), 128)] = c.astype(BF16)
                else:
                    tsin[rows, pl.ds(pl.multiple_of(cb * 128 - 768, 128), 128)] = (-s).astype(BF16)
                c, s = c * tc - s * ts, s * tc + c * ts
            return c, s

        lax.fori_loop(0, SLAB // 256, rotate, (cosines, sines))

    def cosine_column(cb, carry):
        table_column(cb, "cos")
        return carry

    def sine_column(cb, carry):
        table_column(cb, "sin")
        return carry

    lax.fori_loop(0, 6, cosine_column, 0)
    table_column(6, "both")
    lax.fori_loop(7, 13, sine_column, 0)

    known = ids_all.at[pl.ds(0, 13)]
    pltpu.make_async_copy(known, known, id_recv_sem).wait()
    ids_all[RING + 2 * my_z + 1 - my_c] = ids_all[2 * my_y + 1 - my_c]

    def choose(m, carry):
        station = lax.broadcasted_iota(jnp.int32, (STATIONS, 128), 0)
        for line in range(2):
            for side in range(2):
                wanted = ids_all[line * RING + m, side : side + 1, :]
                hot = jnp.transpose(jnp.where(station == wanted, F32(1), F32(0))).astype(BF16)
                for i in range(SHARE // 16):
                    at, pair = i * 32 + side * 16, line * SHARE + i * 16
                    sel[line * RING + m, at : at + 16, :] = hot[pair : pair + 16]
        return carry

    lax.fori_loop(0, RING, choose, 0)

    meta = meta_ref[...]
    square = (128, 128)
    sub, lane = lax.broadcasted_iota(jnp.int32, square, 0), lax.broadcasted_iota(jnp.int32, square, 1)
    dest = meta[3:4, :]
    dest_across = jnp.transpose(jnp.broadcast_to(dest.astype(F32), square)).astype(jnp.int32)
    earlier = (dest_across == dest) & (sub < lane) & (sub < PAIRS)
    position = jnp.sum(jnp.where(earlier, F32(1), F32(0)), axis=0, keepdims=True).astype(jnp.int32)
    counted = (lane[0:1] < PAIRS) & (meta[2:3, :] == 1)
    code = jnp.where(counted, dest * 8 + position * SEGS, -64)

    def place(t, carry):
        target = lax.broadcasted_iota(jnp.int32, (128, 128), 0) + t * 128
        rows = pl.ds(pl.multiple_of(t * 128, 128), 128)
        for k in range(SEGS):
            gsel[rows, k * 128 : (k + 1) * 128] = jnp.where(target == code + k, F32(1), F32(0)).astype(BF16)
        return carry

    lax.fori_loop(0, DEVS * 8 // 128, place, 0)
    slot_across = jnp.transpose(jnp.broadcast_to(meta[4:5, :].astype(F32), square)).astype(BF16)
    for p in range(2):
        corr[p][...] = jnp.zeros_like(corr[p])
    corr[0][3 * 128 :, :128] = slot_across
    corr[0][3 * 128 :, 128:] = slot_across

    places = (my_y, my_z)

    def block(line, k, c):
        return pl.ds(pl.multiple_of((line * RING + 2 * k + c) * SHARE, 16), SHARE)

    steps = [(i, line) for i in (2, 1, 3, 0) for line in range(2)]
    a_copies = [[], []]

    def send_a(p):
        first, width = PIECES[p]
        for n, (i, line) in enumerate(steps):
            k = lax.rem(places[line] + i, 4)
            a_send[p][n] = acc[block(line, k, 1 - my_c), first : first + width].astype(BF16)
            copy = pltpu.make_async_remote_copy(
                src_ref=a_send[p].at[n], dst_ref=a_recv[p].at[n],
                send_sem=a_send_sem.at[p, n], recv_sem=a_recv_sem.at[p, n],
                device_id={"sta": me + 1 - 2 * my_c}, device_id_type=MESH,
            )
            copy.start()
            a_copies[p].append(copy)

    for q in range(PARTS):
        width = WIDTHS[q]
        arrived = wr[q].at[pl.ds(0, MEMBERS - 1)]
        pltpu.make_async_copy(arrived, arrived, w_recv_sem.at[q]).wait()

        def repack(i, carry):
            both = wr[q][pl.ds(2 * i, 2)].astype(F32)
            rows = pl.ds(pl.multiple_of(i * 16, 16), 16)
            low = both[:, :8].reshape(16, width).astype(BF16)
            high = both[:, 8:].reshape(16, width).astype(BF16)
            for j in range(width // 128):
                wc[j, rows, :128] = low[:, j * 128 : (j + 1) * 128]
                wc[j, rows, 128:] = high[:, j * 128 : (j + 1) * 128]
            return carry

        lax.fori_loop(0, MEMBERS // 2, repack, 0)

        def correlate(pair, carry):
            for j in (2 * pair, 2 * pair + 1):
                real_at = pl.ds(pl.multiple_of(j * 128, 128), 128)
                imag_at = pl.ds(pl.multiple_of(WIDE + j * 128, 128), 128)
                for m in range(0, BLOCKS, 8):
                    both = jnp.dot(
                        sel[m : m + 8].reshape(8 * 2 * SHARE, STATIONS), wc[j], preferred_element_type=F32
                    )
                    for i in range(8 * SHARE // 16):
                        a0, a1 = both[i * 32 : i * 32 + 16, :128], both[i * 32 : i * 32 + 16, 128:]
                        b0, b1 = both[i * 32 + 16 : i * 32 + 32, :128], both[i * 32 + 16 : i * 32 + 32, 128:]
                        rows = slice(m * SHARE + i * 16, m * SHARE + i * 16 + 16)
                        cross[rows, real_at] = (a0 * b0 + a1 * b1).astype(BF16)
                        cross[rows, imag_at] = (a1 * b0 - a0 * b1).astype(BF16)
            return carry

        lax.fori_loop(0, width // 256, correlate, 0)

        bins = slice(STARTS[q], STARTS[q] + width)

        def add(columns, value):
            if q == 0:
                acc[:, columns] = value
            else:
                acc[:, columns] += value

        real, imag = cross.at[:, :width], cross.at[:, WIDE : WIDE + width]
        add(slice(896, COLS), jnp.dot(imag[...], tsin[bins, 128:], preferred_element_type=F32))
        if q == PARTS - 1:
            send_a(0)
        add(slice(0, 768), jnp.dot(real[...], tcos[bins, :768], preferred_element_type=F32))
        add(
            slice(768, 896),
            jnp.dot(real[...], tcos[bins, 768:], preferred_element_type=F32)
            + jnp.dot(imag[...], tsin[bins, :128], preferred_element_type=F32),
        )
        if q == PARTS - 1:
            send_a(1)

    b_copies = [[], []]
    for p, (first, width) in enumerate(PIECES):
        for n, (i, line) in enumerate(steps[:6]):
            k = lax.rem(places[line] + i, 4)
            a_copies[p][n].wait_recv()
            mine = acc[block(line, k, my_c), first : first + width]
            b_send[p][n] = (mine + a_recv[p][n].astype(F32)).astype(BF16)
            peer = row + 2 * k + my_c if line == 0 else k * RING + inside
            copy = pltpu.make_async_remote_copy(
                src_ref=b_send[p].at[n], dst_ref=b_recv[p].at[n],
                send_sem=b_send_sem.at[p, n], recv_sem=b_recv_sem.at[p, n],
                device_id={"sta": peer}, device_id_type=MESH,
            )
            copy.start()
            b_copies[p].append(copy)

    scale = F32(BINS ** (-0.5))
    owns = []
    for p, (first, width) in enumerate(PIECES):
        for line in range(2):
            a_copies[p][6 + line].wait_recv()
            for n in range(line, 6, 2):
                b_copies[p][n].wait_recv()
            total = acc[block(line, places[line], my_c), first : first + width]
            total = total + a_recv[p][6 + line].astype(F32)
            for n in range(line, 6, 2):
                total = total + b_recv[p][n].astype(F32)
            total = (total * scale).astype(BF16)
            for k in range(-(-width // SEG)):
                wide = min(SEG, width - k * SEG)
                at = k * 128 + line * SHARE
                corr[p][at : at + SHARE, :wide] = total[:, k * SEG : k * SEG + wide]

        def pack(t, carry):
            rows = pl.ds(pl.multiple_of(t * 256, 256), 256)
            out = jnp.dot(gsel[rows, :], corr[p][...], preferred_element_type=F32)
            c_send[p][pl.ds(t * 32, 32)] = out.reshape(32, 8, SEG).astype(BF16)
            return carry

        lax.fori_loop(0, DEVS // 32, pack, 0)
        own = pltpu.make_async_copy(c_send[p].at[dev], got[p].at[dev], own_sem.at[p])
        own.start()
        owns.append(own)

        def send_row(there, member):
            pltpu.make_async_remote_copy(
                src_ref=c_send[p].at[there * MEMBERS + member], dst_ref=got[p].at[dev],
                send_sem=c_send_sem.at[p], recv_sem=c_recv_sem.at[p],
                device_id={"grp": there, "sta": member}, device_id_type=MESH,
            ).start()

        def route(i, carry):
            member = lax.rem(me + i * 11, MEMBERS)
            for g in (2, 1, 3, 0):
                send_row(lax.rem(grp + g, GROUPS), member)
            return carry

        for g in (2, 1, 3):
            send_row(lax.rem(grp + g, GROUPS), me)
        lax.fori_loop(1, MEMBERS, route, 0)

    for p in range(2):
        for copy in a_copies[p]:
            copy.wait_send()
        for copy in b_copies[p]:
            copy.wait_send()
    pltpu.make_async_copy(known, known, id_send_sem).wait()
    for q in range(PARTS):
        sent = wr[q].at[pl.ds(0, MEMBERS - 1)]
        pltpu.make_async_copy(sent, sent, w_send_sem.at[q]).wait()
    for p in range(2):
        owns[p].wait()
        rest = c_send[p].at[pl.ds(0, DEVS - 1)]
        pltpu.make_async_copy(rest, rest, c_send_sem.at[p]).wait()
        pltpu.make_async_copy(rest, rest, c_recv_sem.at[p]).wait()


def correlate_and_route(*operands):
    vmem = pl.BlockSpec(memory_space=pltpu.VMEM)
    dma = pltpu.SemaphoreType.DMA
    return pl.pallas_call(
        main_kernel,
        out_shape=[jax.ShapeDtypeStruct((DEVS, 8, SEG), BF16)] * 2,
        in_specs=[pl.BlockSpec(memory_space=pltpu.HBM), vmem],
        out_specs=[pl.BlockSpec(memory_space=pl.ANY)] * 2,
        scratch_shapes=[
            *[pltpu.VMEM((RING, 16, w), BF16) for w in WIDTHS],
            *[pltpu.VMEM((MEMBERS, 16, w), BF16) for w in WIDTHS],
            pltpu.VMEM((RING, 2, BINS), F32),
            pltpu.VMEM((WIDE // 128, STATIONS, 256), BF16),
            pltpu.VMEM((BLOCKS, 8, 128), jnp.int32),
            pltpu.VMEM((BLOCKS, 2 * SHARE, STATIONS), BF16),
            pltpu.VMEM((SLAB, 896), BF16),
            pltpu.VMEM((SLAB, 896), BF16),
            pltpu.VMEM((RING * PAIRS, COLS), F32),
            pltpu.VMEM((RING * PAIRS, 2 * WIDE), BF16),
            *[pltpu.VMEM((8, SHARE, w), BF16) for _ in range(2) for _, w in PIECES],
            *[pltpu.VMEM((6, SHARE, w), BF16) for _ in range(2) for _, w in PIECES],
            *[pltpu.VMEM((SEGS * 128, SEG), BF16) for _ in range(2)],
            pltpu.VMEM((DEVS * 8, SEGS * 128), BF16),
            *[pltpu.VMEM((DEVS, 8, SEG), BF16) for _ in range(2)],
            dma, dma,
            dma((PARTS,)), dma((PARTS,)),
            dma((2, 8)), dma((2, 8)),
            dma((2, 6)), dma((2, 6)),
            dma((2,)), dma((2,)), dma((2,)), dma((RING,)),
        ],
        compiler_params=pltpu.CompilerParams(
            collective_id=0, has_side_effects=True, vmem_limit_bytes=52 * 1024 * 1024
        ),
    )(*operands)


def stack_kernel(got_a, got_b, stacks_ref, out_ref):
    rows = DEVS * 8
    got = [ref[...].reshape(rows, SEG) for ref in (got_a, got_b)]
    first = jnp.where(lax.broadcasted_iota(jnp.int32, (8, SEG), 1) == 0, F32(1), F32(0)).astype(BF16)
    marks = lax.dot_general(first, got[0], (((1,), (1,)), ((), ())), preferred_element_type=F32)
    place = lax.broadcasted_iota(jnp.int32, (8, rows), 1) & 3
    marks = jnp.where(place == 3, marks, F32(0))
    marks = jnp.maximum(marks, pltpu.roll(marks, rows - 1, 1))
    marks = jnp.maximum(marks, pltpu.roll(marks, rows - 2, 1))
    code = (marks.astype(jnp.int32) + place * PAIRS)[0:1]
    want = lax.broadcasted_iota(jnp.int32, (SEGS * PAIRS, rows), 0)
    hot = jnp.where(want == code, F32(1), F32(0)).astype(BF16)
    near, far = [jnp.dot(hot, g, preferred_element_type=F32) for g in (got[1], got[0])]
    parts = [near[k * PAIRS : (k + 1) * PAIRS] for k in range(SEGS)]
    parts += [far[k * PAIRS : (k + 1) * PAIRS] for k in range(SEGS - 1)]
    sums = jnp.concatenate(parts, axis=1)
    even, odd = sums[:, :896], sums[:, SIDE : SIDE + 896]
    tiles = 7
    gap = even - odd
    high = gap.astype(BF16)
    low = (gap - high.astype(F32)).astype(BF16)
    stack = jnp.concatenate(
        [v[:, t * 128 : (t + 1) * 128] for v in (high, low) for t in range(tiles)], axis=0
    )
    mirror = lax.broadcasted_iota(jnp.int32, (128, 128), 0) + lax.broadcasted_iota(jnp.int32, (128, 128), 1)
    mirror = jnp.where(mirror == 127, F32(1), F32(0)).astype(BF16)
    turned = jnp.dot(stack, mirror, preferred_element_type=F32)
    turned = turned[: tiles * PAIRS] + turned[tiles * PAIRS :]
    behind = jnp.concatenate(
        [turned[t * PAIRS : (t + 1) * PAIRS] for t in reversed(range(tiles))], axis=1
    )
    skip = tiles * 128 - HALF
    out_ref[:, :HALF] = stacks_ref[:, :HALF] + behind[:, skip:]
    out_ref[:, HALF:] = stacks_ref[:, HALF:] + (even + odd)[:, 1:HALF]


def add_rows(got_a, got_b, stacks):
    vmem = pl.BlockSpec(memory_space=pltpu.VMEM)
    return pl.pallas_call(
        stack_kernel,
        out_shape=jax.ShapeDtypeStruct(stacks.shape, F32),
        in_specs=[vmem] * 3,
        out_specs=vmem,
        compiler_params=pltpu.CompilerParams(vmem_limit_bytes=40 * 1024 * 1024),
    )(got_a, got_b, stacks)


def local(spectra, stacks, pair_sta, pair_valid, owner, slot):
    rows = [pair_sta, pair_valid[None, :], owner.reshape(1, PAIRS), slot[None, :]]
    meta = jnp.pad(jnp.concatenate(rows, axis=0), ((0, 3), (0, 128 - PAIRS)))
    got_a, got_b = correlate_and_route(spectra, meta)
    return add_rows(got_a, got_b, stacks)


def solution(mesh):
    return jax.shard_map(
        local,
        mesh=mesh,
        in_specs=(
            P(("grp", "sta"), None, None),
            P(("grp", "sta"), None),
            P(None, ("grp", "sta")),
            P(("grp", "sta")),
            P(("grp", "sta"), None),
            P(("grp", "sta")),
        ),
        out_specs=P(("grp", "sta"), None),
        check_vma=False,
    )
```
